512 devices in a mesh: tile: 256 (over z, y, x), depth: 2 (over core).
Axes of the slice: x: 4, y: 8, z: 8, core: 2. Of those that a mesh axis runs over, the one named last changes fastest.
Arguments:
- density: float32 [64, 4096, 256], P('depth', 'tile'), may hold values from -6 to 6
- absorption: float32 [4096, 256], P('tile'), may hold values from 0.25 to 32
- view_dir: int32 [4096], P('tile'), may hold values 0 or 1
- target_ids: int32 [4096, 256], P('tile'), may hold values from 0 to 127
- palette: float32 [3, 128], replicated, may hold values from -3 to 3
- emission_coef: float32 [3, 4], replicated, may hold values from -3 to 3
- light: float32 [3], replicated, may hold values from -4 to 4
Outputs:
- image: float32 [3, 4096, 256], P(None, ('tile', 'depth'))
- density_grad: float32 [64, 4096, 256], P('depth', 'tile')
The draws below stay inside these ranges and needn't reach their ends.
All inputs are finite; a program needn't handle non-finite values. No bound on the sum of `view_dir` on one device may be relied on, other than what follows from the above.
Results may differ from the reference program's by a relative error of at most 0.00023.
Values sent between devices are 32-bit elements; how exact they have to be, the bound alone decides.
A program may use at most 64 MiB of HBM per device.

```python
import math
import jax
import jax.numpy as jnp
import numpy as np
from jax import lax

COLS = 256
PALETTE = 128
NZ = 64
NY = 4096


def set_ends(drawn, key, smallest, top_value):
    longest = drawn.shape.index(max(drawn.shape))
    spots = []
    for shift in (0, 1):
        where = [jax.random.randint(jax.random.fold_in(key, axis), (), 0, length) for axis, length in enumerate(drawn.shape)]
        where[longest] = (where[longest] + shift) % drawn.shape[longest]
        spots.append(tuple(where))
    return drawn.at[spots[0]].set(smallest).at[spots[1]].set(top_value)


def shard_levels(own_key, shape, shards, low, high):
    loudness = 1.0
    for dim, shards_of in shards:
        steps = jax.random.uniform(jax.random.fold_in(jax.random.fold_in(own_key, 6), dim), (shards_of,), jnp.float32, low / len(shards), high / len(shards))
        loudness = loudness * jnp.repeat(jnp.exp(steps), shape[dim] // shards_of).reshape((-1,) + (1,) * (len(shape) - 1 - dim))
    return loudness


def cumulative_ranks(number_of, skew):
    loads = [(1 << 20) // math.isqrt(standing ** skew) + 1 for standing in range(1, number_of + 1)]
    scale = 1 + sum(loads) // (1 << 30)
    return np.cumsum(np.array([max(1, weight // scale) for weight in loads]))


def skewed_ids(rng, dims, count, slope):
    grid = cumulative_ranks(count, slope)
    ticket = jax.random.randint(jax.random.fold_in(rng, 1), dims, 0, int(grid[count - 1]))
    standing = jnp.searchsorted(jnp.asarray(grid, jnp.int32), ticket, side="right")
    return jax.random.permutation(jax.random.fold_in(rng, 2), count)[standing].astype(jnp.int32)


def bell_draw(rng, extent, width, most, pieces=(), dtype=jnp.bfloat16):
    entries = width * jax.random.normal(rng, extent, jnp.float32)
    if pieces:
        entries = entries * shard_levels(rng, extent, pieces, -0.22, 0.18)
    return jnp.clip(entries, -most, most).astype(dtype)


def setup_inputs(seed: int = 0) -> dict:
    key_of = jax.random.split(jax.random.key(seed), 8)
    density = bell_draw(key_of[0], (NZ, NY, COLS), 1.0, 6.0, ((0, 2), (1, 256)), jnp.float32)
    absorption = jnp.clip(jnp.exp(math.log(32.0) - 4.8520303 * jax.random.uniform(key_of[1], (NY, COLS), jnp.float32) ** shard_levels(key_of[1], (NY, COLS), ((0, 256),), -0.2, 0.2)), 0.25, 32.0)
    view_dir = set_ends((jax.random.randint(key_of[2], (NY,), 0, 2) < 1).astype(jnp.int32), jax.random.fold_in(key_of[2], 1), 0, 1)
    target_ids = set_ends(skewed_ids(key_of[3], (NY, COLS), PALETTE, 2), jax.random.fold_in(key_of[3], 3), 0, PALETTE - 1).astype(jnp.int32)
    palette = bell_draw(key_of[4], (3, PALETTE), 0.5, 3.0, (), jnp.float32)
    emission_coef = bell_draw(key_of[5], (3, 4), 0.5, 3.0, (), jnp.float32)
    light = bell_draw(key_of[6], (3,), 1.0, 4.0, (), jnp.float32)
    return dict(density=density, absorption=absorption, view_dir=view_dir, target_ids=target_ids, palette=palette, emission_coef=emission_coef, light=light)


def smooth_field(ext):
    core = ext[1:-1, 1:-1]
    total = 2.0 * core + ext[2:, 1:-1] + ext[:-2, 1:-1] + ext[1:-1, 2:] + ext[1:-1, :-2]
    total = total + jnp.roll(core, -1, 2) + jnp.roll(core, 1, 2)
    return total / 8.0

def shade_parts(padded, absorption, emission_coef, light, depth_count):
    smoothed = smooth_field(padded)
    centre = smoothed[1:-1, 1:-1]
    grad_z = 0.5 * (smoothed[2:, 1:-1] - smoothed[:-2, 1:-1])
    grad_y = 0.5 * (smoothed[1:-1, 2:] - smoothed[1:-1, :-2])
    grad_x = 0.5 * (jnp.roll(centre, -1, 2) - jnp.roll(centre, 1, 2))
    facing = grad_z * light[0] + grad_y * light[1] + grad_x * light[2]
    shade = 0.5 + 0.5 * facing / jnp.sqrt(1.0 + grad_z * grad_z + grad_y * grad_y + grad_x * grad_x)
    value = emission_coef[:, 3][:, None, None, None] * centre[None] + emission_coef[:, 2][:, None, None, None]
    value = value * centre[None] + emission_coef[:, 1][:, None, None, None]
    value = value * centre[None] + emission_coef[:, 0][:, None, None, None]
    emission = value * shade[None]
    sigma = absorption[None] * jax.nn.softplus(centre) / depth_count
    return (emission, sigma)

def reference(density, absorption, view_dir, target_ids, palette, emission_coef, light):
    depth_count = density.shape[0]
    flipped = (view_dir == 1)[None, :, None]

    def render(field):
        padded = jnp.pad(field, ((2, 2), (2, 2), (0, 0)))
        emission, sigma = shade_parts(padded, absorption, emission_coef, light, depth_count)
        ascending = jnp.cumsum(sigma, 0) - sigma
        total = lax.optimization_barrier(jnp.sum(sigma, 0))
        descending = total[None] - ascending - sigma
        depth_before = jnp.where(flipped, descending, ascending)
        weight = jnp.exp(-depth_before) * (1.0 - jnp.exp(-sigma))
        return lax.optimization_barrier(jnp.sum(emission * weight[None], 1))
    image, pullback = jax.vjp(render, density)
    target = palette[:, target_ids]
    density_grad, = pullback((image - target) * depth_count)
    return (image, density_grad)
```

```python
import functools
import math

import jax
import jax.numpy as jnp
from jax import lax
from jax.experimental import pallas as pl
from jax.experimental.pallas import tpu as pltpu
from jax.sharding import PartitionSpec as P

MESH = pl.DeviceIdType.MESH
LOG2E = math.log2(math.e)
CHUNKS = 4


def body(
    tiles, slab, rows, cols, depth_count,
    density, absorption, view_dir, target_ids, palette, coef, light,
    image_out, grad_out,
    field, smooth, shade_b, cz_b, cy_b, cx_b, fac_b, edge_b, ay_b, qz_b, full_b, grad_b,
    ab_v, ids_v, pal_v, view_s, coef_s, light_s, image_v, mine, theirs, tgt_v,
    back_y, back_z, back_d,
    load_sem, small_sem, halo_send, halo_recv, face_send, face_recv, mid_send, mid_recv,
    ret_send, ret_recv, out_sem,
):
    tile = lax.axis_index("tile")
    core = lax.axis_index("depth")
    other = 1 - core
    has_prev = tile > 0
    has_next = tile < tiles - 1
    ext = rows + 8
    step = slab // CHUNKS
    sign = 2 * core - 1
    first = (1 - core) * (slab - 1)

    def layer(k):
        return first + sign * k

    def chunk_start(i):
        return core * (step * i) + other * (slab - step - step * i)

    prev_id = (jnp.maximum(tile - 1, 0), core)
    next_id = (jnp.minimum(tile + 1, tiles - 1), core)
    across_id = (tile, other)
    prev_across = (jnp.maximum(tile - 1, 0), other)
    next_across = (jnp.minimum(tile + 1, tiles - 1), other)

    def rx(value, shift):
        return pltpu.roll(value, shift % cols, 1)

    def ry(value, shift):
        return pltpu.roll(value, shift % ext, 0)

    own = pltpu.make_async_copy(density, field.at[pl.ds(2, slab), pl.ds(0, rows), :], load_sem)
    own.start()
    smalls = [
        pltpu.make_async_copy(src, dst, small_sem.at[n])
        for n, (src, dst) in enumerate(
            [(view_dir, view_s), (absorption, ab_v), (light, light_s), (coef, coef_s), (target_ids, ids_v), (palette, pal_v)]
        )
    ]
    for copy in smalls:
        copy.start()

    zero_layer = jnp.zeros((ext, cols), jnp.float32)
    back_d[0] = jnp.zeros((8, cols), jnp.float32)

    field[2 + layer(slab)] = zero_layer

    @pl.when(jnp.logical_not(has_prev))
    def _():
        def clear(j, carry):
            field[j, pl.ds(rows + 6, 2), :] = jnp.zeros((2, cols), jnp.float32)
            return carry

        lax.fori_loop(0, slab + 4, clear, 0)

        def clear_back(j, carry):
            back_y[j, pl.ds(0, 2), :] = jnp.zeros((2, cols), jnp.float32)
            return carry

        lax.fori_loop(0, slab, clear_back, 0)

    @pl.when(jnp.logical_not(has_next))
    def _():
        def clear(j, carry):
            field[j, pl.ds(rows, 2), :] = jnp.zeros((2, cols), jnp.float32)
            return carry

        lax.fori_loop(0, slab + 4, clear, 0)

        def clear_back(j, carry):
            back_y[j, pl.ds(6, 2), :] = jnp.zeros((2, cols), jnp.float32)
            return carry

        lax.fori_loop(0, slab, clear_back, 0)

    barrier = pltpu.get_barrier_semaphore()
    pl.semaphore_signal(barrier, inc=1, device_id=across_id, device_id_type=MESH)

    @pl.when(has_prev)
    def _():
        pl.semaphore_signal(barrier, inc=1, device_id=prev_id, device_id_type=MESH)
        pl.semaphore_signal(barrier, inc=1, device_id=prev_across, device_id_type=MESH)

    @pl.when(has_next)
    def _():
        pl.semaphore_signal(barrier, inc=1, device_id=next_id, device_id_type=MESH)
        pl.semaphore_signal(barrier, inc=1, device_id=next_across, device_id_type=MESH)

    pl.semaphore_wait(barrier, 1 + 2 * has_prev.astype(jnp.int32) + 2 * has_next.astype(jnp.int32))

    face = pltpu.make_async_remote_copy(
        density.at[pl.ds(other * (slab - 2), 2)],
        field.at[pl.ds(core * (slab + 2), 2), pl.ds(0, rows), :],
        face_send.at[0], face_recv.at[0], device_id=across_id, device_id_type=MESH,
    )
    face_z = other * (slab - 1)
    face_at = 2 + core * slab - other
    corner_prev = pltpu.make_async_remote_copy(
        density.at[pl.ds(face_z, 1), pl.ds(0, 1), :],
        field.at[pl.ds(face_at, 1), pl.ds(rows, 1), :],
        face_send.at[1], face_recv.at[1], device_id=prev_across, device_id_type=MESH,
    )
    corner_next = pltpu.make_async_remote_copy(
        density.at[pl.ds(face_z, 1), pl.ds(rows - 1, 1), :],
        field.at[pl.ds(face_at, 1), pl.ds(rows + 7, 1), :],
        face_send.at[2], face_recv.at[2], device_id=next_across, device_id_type=MESH,
    )

    def halo_prev(i):
        start = chunk_start(i)
        return pltpu.make_async_remote_copy(
            density.at[pl.ds(start, step), pl.ds(0, 2), :],
            field.at[pl.ds(2 + start, step), pl.ds(rows, 2), :],
            halo_send.at[0, i], halo_recv.at[0, i], device_id=prev_id, device_id_type=MESH,
        )

    def halo_next(i):
        start = chunk_start(i)
        return pltpu.make_async_remote_copy(
            density.at[pl.ds(start, step), pl.ds(rows - 2, 2), :],
            field.at[pl.ds(2 + start, step), pl.ds(rows + 6, 2), :],
            halo_send.at[1, i], halo_recv.at[1, i], device_id=next_id, device_id_type=MESH,
        )

    face.start()

    @pl.when(has_prev)
    def _():
        corner_prev.start()

    @pl.when(has_next)
    def _():
        corner_next.start()

    for i in range(CHUNKS):

        @pl.when(has_prev)
        def _(i=i):
            halo_prev(i).start()

        @pl.when(has_next)
        def _(i=i):
            halo_next(i).start()

    for copy in smalls:
        copy.wait()
    row_of = lax.broadcasted_iota(jnp.int32, (rows, cols), 0)
    view = jnp.zeros((rows, cols), jnp.int32)
    for y in range(rows):
        view = jnp.where(row_of == y, view_s[y], view)
    ascending = view == other
    absorb = ab_v[...]
    half_light = [0.5 * light_s[0] * sign.astype(jnp.float32), 0.5 * light_s[1], 0.5 * light_s[2]]
    for c in range(3):
        table = jnp.broadcast_to(pal_v[pl.ds(c, 1), :], (8, pal_v.shape[1]))
        for y in range(0, rows, 8):
            for x in range(0, cols, 128):
                picked = jnp.take_along_axis(table, ids_v[pl.ds(y, 8), pl.ds(x, 128)], axis=1, mode="promise_in_bounds")
                tgt_v[c, pl.ds(y, 8), pl.ds(x, 128)] = picked

    own.wait()
    face.wait_recv()

    @pl.when(has_prev)
    def _():
        corner_next.wait_recv()

    @pl.when(has_next)
    def _():
        corner_prev.wait_recv()

    def blur(k):
        at = 2 + layer(k)
        here = field[at]
        total = 2.0 * here + field[at - 1] + field[at + 1]
        total = total + (ry(here, 1) + ry(here, -1)) + (rx(here, 1) + rx(here, -1))
        smooth[k + 1] = total

    scale = absorb * (LOG2E / depth_count)
    slope = absorb * (1.0 / (8.0 * depth_count))

    def shade(k, depth):
        here = smooth[k + 1]
        mid = here[:rows]
        dz = smooth[k + 2, pl.ds(0, rows), :] - smooth[k, pl.ds(0, rows), :]
        dy = ry(here, -1)[:rows] - ry(here, 1)[:rows]
        dx = rx(mid, -1) - rx(mid, 1)
        inv = lax.rsqrt(256.0 + dz * dz + dy * dy + dx * dx)
        facing = (half_light[0] * dz + half_light[1] * dy + half_light[2] * dx) * inv
        bend = facing * inv
        shade_b[k] = 0.5 + facing
        cz_b[k] = inv * (half_light[0] - bend * dz)
        cy_b[k] = inv * (half_light[1] - bend * dy)
        cx_b[k] = inv * (half_light[2] - bend * dx)
        power = mid * (LOG2E / 8.0)
        plus = jnp.log(1.0 + lax.exp2(power))
        fac_b[k] = slope * lax.exp2(power - plus * LOG2E)
        edge_b[k] = depth
        return depth + scale * plus

    def run(lo, count, unroll, one, carry):
        def several(j, carry):
            for u in range(unroll):
                carry = one(lo + j * unroll + u, carry)
            return carry

        return lax.fori_loop(0, count // unroll, several, carry)

    def blur_one(k, carry):
        blur(k)
        return carry

    depth = jnp.zeros((rows, cols), jnp.float32)
    for i in range(CHUNKS):

        @pl.when(has_prev)
        def _(i=i):
            halo_next(i).wait_recv()

        @pl.when(has_next)
        def _(i=i):
            halo_prev(i).wait_recv()

        run(step * i - 1, step, 2, blur_one, 0)
        if i:
            depth = run(step * (i - 1), step, 2, shade, depth)
    blur(slab - 1)
    smooth[slab + 1] = field[2 + layer(slab - 1)]
    depth = run(slab - step, step, 2, shade, depth)

    toward = jnp.where(ascending, -1.0, 1.0)
    base = jnp.where(ascending, 0.0, -depth)

    def composite(k, carry):
        left, m0, m1, m2, m3 = carry
        right = lax.exp2(toward * edge_b[k + 1] + base)
        mid = smooth[k + 1, pl.ds(0, rows), :]
        part = jnp.abs(left - right) * shade_b[k]
        m0 = m0 + part
        part = part * mid
        m1 = m1 + part
        part = part * mid
        m2 = m2 + part
        part = part * mid
        m3 = m3 + part
        edge_b[k] = left
        return (right, m0, m1, m2, m3)

    edge_b[slab] = depth
    zero = jnp.zeros((rows, cols), jnp.float32)
    left = lax.exp2(base)
    right, m0, m1, m2, m3 = run(0, slab, 2, composite, (left, zero, zero, zero, zero))
    edge_b[slab] = right
    for c in range(3):
        mine[c] = coef_s[c, 0] * m0 + (coef_s[c, 1] / 8.0) * m1 + (coef_s[c, 2] / 64.0) * m2 + (coef_s[c, 3] / 512.0) * m3
    mine[3] = depth
    swap = pltpu.make_async_remote_copy(
        mine, theirs, mid_send, mid_recv, device_id=across_id, device_id_type=MESH
    )
    swap.start()
    swap.wait()

    enter = jnp.where(ascending, lax.exp2(-theirs[3]), 1.0)
    leave = lax.exp2(-depth)
    misfit = []
    before = jnp.zeros((rows, cols), jnp.float32)
    for c in range(3):
        colour = jnp.where(ascending, theirs[c] + enter * mine[c], mine[c] + leave * theirs[c])
        image_v[c] = colour
        gap = (colour - tgt_v[c]) * float(depth_count)
        misfit.append(gap)
        before = before + gap * jnp.where(ascending, mine[c], theirs[c])
    rest = jnp.where(ascending, enter, leave) * before
    share = rows // 2
    image_copy = pltpu.make_async_copy(
        image_v.at[:, pl.ds(pl.multiple_of(core * share, 8), share), :], image_out, out_sem.at[CHUNKS]
    )
    image_copy.start()
    ramp = [
        enter
        * (misfit[0] * coef_s[0, i] + misfit[1] * coef_s[1, i] + misfit[2] * coef_s[2, i])
        * (1.0 / 8.0**i)
        for i in range(4)
    ]
    ramp2 = 2.0 * ramp[2]
    ramp3 = 3.0 * ramp[3]
    blank = jnp.zeros((8, cols), jnp.float32)

    def pull(k, rest):
        left = edge_b[k]
        signed = left - edge_b[k + 1]
        weight = jnp.abs(signed)
        mid = smooth[k + 1, pl.ds(0, rows), :]
        lit = shade_b[k]
        value = ramp[0] + mid * (ramp[1] + mid * (ramp[2] + mid * ramp[3]))
        deriv = ramp[1] + mid * (ramp2 + mid * ramp3)
        shown = lit * value
        pulled = weight * value
        direct = weight * lit * deriv + (left * shown - rest) * fac_b[k]
        qx = pulled * cx_b[k]
        qy = jnp.concatenate([pulled * cy_b[k], blank], 0)
        direct = direct + rx(qx, 1) - rx(qx, -1)
        ay_b[k] = ry(qy, 1) - ry(qy, -1) + jnp.concatenate([direct, blank], 0)
        qz_b[k + 1] = pulled * cz_b[k]
        return rest - signed * shown

    def gather(k, carry):
        full_b[k + 2, pl.ds(0, rows), :] = ay_b[k, pl.ds(0, rows), :] + qz_b[k] - qz_b[k + 2]
        full_b[k + 2, pl.ds(rows, 8), :] = ay_b[k, pl.ds(rows, 8), :]
        return carry

    def spread(k, carry):
        here = full_b[k + 2]
        total = 2.0 * here + full_b[k + 1] + full_b[k + 3]
        total = total + (ry(here, 1) + ry(here, -1)) + (rx(here, 1) + rx(here, -1))
        grad_b[2 + layer(k)] = total
        return carry

    def back_prev(i):
        start = chunk_start(i)
        return pltpu.make_async_remote_copy(
            grad_b.at[pl.ds(2 + start, step), pl.ds(rows + 6, 2), :],
            back_y.at[pl.ds(start, step), pl.ds(6, 2), :],
            ret_send.at[0, i], ret_recv.at[0, i], device_id=prev_id, device_id_type=MESH,
        )

    def back_next(i):
        start = chunk_start(i)
        return pltpu.make_async_remote_copy(
            grad_b.at[pl.ds(2 + start, step), pl.ds(rows, 2), :],
            back_y.at[pl.ds(start, step), pl.ds(0, 2), :],
            ret_send.at[1, i], ret_recv.at[1, i], device_id=next_id, device_id_type=MESH,
        )

    back_face = pltpu.make_async_remote_copy(
        grad_b.at[pl.ds(other * (slab + 2), 2), pl.ds(0, rows), :],
        back_z,
        face_send.at[3], face_recv.at[3], device_id=across_id, device_id_type=MESH,
    )
    back_corner_prev = pltpu.make_async_remote_copy(
        grad_b.at[face_ext(core, slab), pl.ds(rows + 7, 1), :],
        back_d.at[:, pl.ds(7, 1), :],
        face_send.at[4], face_recv.at[4], device_id=prev_across, device_id_type=MESH,
    )
    back_corner_next = pltpu.make_async_remote_copy(
        grad_b.at[face_ext(core, slab), pl.ds(rows, 1), :],
        back_d.at[:, pl.ds(0, 1), :],
        face_send.at[5], face_recv.at[5], device_id=next_across, device_id_type=MESH,
    )

    def send_back(i):
        @pl.when(has_prev)
        def _():
            back_prev(i).start()

        @pl.when(has_next)
        def _():
            back_next(i).start()

    qz_b[0] = zero
    qz_b[slab + 1] = zero
    for i in range(CHUNKS):
        rest = run(step * i, step, 2, pull, rest)
        if i == 0:
            full_b[0] = zero_layer
            full_b[1, pl.ds(0, rows), :] = -qz_b[1]
            full_b[1, pl.ds(rows, 8), :] = blank
            run(0, step - 1, 1, gather, 0)
            spread(-1, 0)
            grad_b[2 + layer(-2), pl.ds(0, rows), :] = full_b[1, pl.ds(0, rows), :]
            back_face.start()

            @pl.when(has_prev)
            def _():
                back_corner_prev.start()

            @pl.when(has_next)
            def _():
                back_corner_next.start()
        else:
            run(step * i - 1, step, 2, gather, 0)
            run(step * (i - 1), step, 2, spread, 0)
            send_back(i - 1)
    gather(slab - 1, 0)
    full_b[slab + 2, pl.ds(0, rows), :] = qz_b[slab]
    full_b[slab + 2, pl.ds(rows, 8), :] = blank
    run(slab - step, step, 2, spread, 0)
    send_back(CHUNKS - 1)

    row8 = lax.broadcasted_iota(jnp.int32, (8, cols), 0)

    def add(k, carry):
        z = layer(k)
        more = back_y[z]
        grad_b[2 + z, pl.ds(0, 8), :] = grad_b[2 + z, pl.ds(0, 8), :] + jnp.where(row8 < 2, more, 0.0)
        grad_b[2 + z, pl.ds(rows - 8, 8), :] = grad_b[2 + z, pl.ds(rows - 8, 8), :] + jnp.where(row8 > 5, more, 0.0)
        return carry

    outs = []
    for i in range(CHUNKS):
        start = chunk_start(i)
        if i == 0:
            back_face.wait_recv()

            @pl.when(has_prev)
            def _():
                back_corner_next.wait_recv()

            @pl.when(has_next)
            def _():
                back_corner_prev.wait_recv()

            near = 2 + layer(0)
            grad_b[near, pl.ds(0, rows), :] = grad_b[near, pl.ds(0, rows), :] + back_z[face_ext_in(core)]
            grad_b[near, pl.ds(0, 8), :] = grad_b[near, pl.ds(0, 8), :] + jnp.where(row8 < 1, back_d[0], 0.0)
            grad_b[near, pl.ds(rows - 8, 8), :] = grad_b[near, pl.ds(rows - 8, 8), :] + jnp.where(row8 > 6, back_d[0], 0.0)
            near = 2 + layer(1)
            grad_b[near, pl.ds(0, rows), :] = grad_b[near, pl.ds(0, rows), :] + back_z[1 - face_ext_in(core)]

        @pl.when(has_prev)
        def _(i=i):
            back_next(i).wait_recv()

        @pl.when(has_next)
        def _(i=i):
            back_prev(i).wait_recv()

        @pl.when(has_prev)
        def _(i=i):
            back_prev(i).wait_send()

        @pl.when(has_next)
        def _(i=i):
            back_next(i).wait_send()

        run(step * i, step, 2, add, 0)
        out = pltpu.make_async_copy(
            grad_b.at[pl.ds(2 + start, step), pl.ds(0, rows), :], grad_out.at[pl.ds(start, step)], out_sem.at[i]
        )
        out.start()
        outs.append(out)

    face.wait_send()
    back_face.wait_send()

    @pl.when(has_prev)
    def _():
        corner_prev.wait_send()
        back_corner_prev.wait_send()
        for i in range(CHUNKS):
            halo_prev(i).wait_send()

    @pl.when(has_next)
    def _():
        corner_next.wait_send()
        back_corner_next.wait_send()
        for i in range(CHUNKS):
            halo_next(i).wait_send()

    image_copy.wait()
    for out in outs:
        out.wait()


def face_ext(core, slab):
    return pl.ds(core * 1 + (1 - core) * (slab + 2), 1)


def face_ext_in(core):
    return 1 - core


def solution(mesh):
    tiles = mesh.shape["tile"]

    def shards(density, absorption, view_dir, target_ids, palette, coef, light):
        slab, rows, cols = density.shape
        ext = rows + 8
        f32 = jnp.float32
        kernel = functools.partial(body, tiles, slab, rows, cols, 2 * slab)
        scratch = [
            pltpu.VMEM((slab + 4, ext, cols), f32),
            pltpu.VMEM((slab + 2, ext, cols), f32),
            *[pltpu.VMEM((slab, rows, cols), f32)] * 5,
            pltpu.VMEM((slab + 1, rows, cols), f32),
            pltpu.VMEM((slab, ext, cols), f32),
            pltpu.VMEM((slab + 2, rows, cols), f32),
            pltpu.VMEM((slab + 3, ext, cols), f32),
            pltpu.VMEM((slab + 4, ext, cols), f32),
            pltpu.VMEM(absorption.shape, f32),
            pltpu.VMEM(target_ids.shape, jnp.int32),
            pltpu.VMEM(palette.shape, f32),
            pltpu.SMEM(view_dir.shape, jnp.int32),
            pltpu.SMEM(coef.shape, f32),
            pltpu.SMEM(light.shape, f32),
            pltpu.VMEM((3, rows, cols), f32),
            pltpu.VMEM((4, rows, cols), f32),
            pltpu.VMEM((4, rows, cols), f32),
            pltpu.VMEM((3, rows, cols), f32),
            pltpu.VMEM((slab, 8, cols), f32),
            pltpu.VMEM((2, rows, cols), f32),
            pltpu.VMEM((1, 8, cols), f32),
            pltpu.SemaphoreType.DMA,
            pltpu.SemaphoreType.DMA((6,)),
            pltpu.SemaphoreType.DMA((2, CHUNKS)),
            pltpu.SemaphoreType.DMA((2, CHUNKS)),
            pltpu.SemaphoreType.DMA((6,)),
            pltpu.SemaphoreType.DMA((6,)),
            pltpu.SemaphoreType.DMA,
            pltpu.SemaphoreType.DMA,
            pltpu.SemaphoreType.DMA((2, CHUNKS)),
            pltpu.SemaphoreType.DMA((2, CHUNKS)),
            pltpu.SemaphoreType.DMA((CHUNKS + 1,)),
        ]
        return pl.pallas_call(
            kernel,
            out_shape=(
                jax.ShapeDtypeStruct((3, rows // 2, cols), f32),
                jax.ShapeDtypeStruct(density.shape, f32),
            ),
            in_specs=[pl.BlockSpec(memory_space=pl.ANY)] * 7,
            out_specs=[pl.BlockSpec(memory_space=pl.ANY)] * 2,
            scratch_shapes=scratch,
            compiler_params=pltpu.CompilerParams(
                collective_id=0, has_side_effects=True, vmem_limit_bytes=24 * 1024 * 1024
            ),
            cost_estimate=pl.CostEstimate(flops=200 * slab * rows * cols, bytes_accessed=8 * slab * rows * cols, transcendentals=0),
        )(density, absorption, view_dir, target_ids, palette, coef, light)

    placed = (P("depth", "tile", None), P("tile", None), P("tile"), P("tile", None), P(), P(), P())
    return jax.shard_map(
        shards,
        mesh=mesh,
        in_specs=placed,
        out_specs=(P(None, ("tile", "depth"), None), P("depth", "tile", None)),
        check_vma=False,
    )
```

```python
import functools
import math

import jax
import jax.numpy as jnp
from jax import lax
from jax.experimental import pallas as pl
from jax.experimental.pallas import tpu as pltpu
from jax.sharding import PartitionSpec as P

MESH = pl.DeviceIdType.MESH
LOG2E = math.log2(math.e)
CHUNKS = 4


def body(
    tiles, slab, rows, cols, depth_count,
    density, absorption, view_dir, target_ids, palette, coef, light,
    image_out, grad_out,
    field, smooth, shade_b, cz_b, cy_b, cx_b, fac_b, edge_b, ay_b, qz_b, full_b, grad_b,
    ab_v, ids_v, pal_v, view_s, coef_s, light_s, image_v, mine, theirs, tgt_v,
    back_y, back_z, back_d,
    load_sem, small_sem, halo_send, halo_recv, face_send, face_recv, mid_send, mid_recv,
    ret_send, ret_recv, out_sem,
):
    tile = lax.axis_index("tile")
    core = lax.axis_index("depth")
    other = 1 - core
    has_prev = tile > 0
    has_next = tile < tiles - 1
    ext = rows + 8
    step = slab // CHUNKS
    sign = 2 * core - 1
    first = (1 - core) * (slab - 1)

    def layer(k):
        return first + sign * k

    def chunk_start(i):
        return core * (step * i) + other * (slab - step - step * i)

    prev_id = (jnp.maximum(tile - 1, 0), core)
    next_id = (jnp.minimum(tile + 1, tiles - 1), core)
    across_id = (tile, other)
    prev_across = (jnp.maximum(tile - 1, 0), other)
    next_across = (jnp.minimum(tile + 1, tiles - 1), other)

    def rx(value, shift):
        return pltpu.roll(value, shift % cols, 1)

    def ry(value, shift):
        return pltpu.roll(value, shift % ext, 0)

    own = pltpu.make_async_copy(density, field.at[pl.ds(2, slab), pl.ds(0, rows), :], load_sem)
    own.start()
    smalls = [
        pltpu.make_async_copy(src, dst, small_sem.at[n])
        for n, (src, dst) in enumerate(
            [(view_dir, view_s), (absorption, ab_v), (light, light_s), (coef, coef_s), (target_ids, ids_v), (palette, pal_v)]
        )
    ]
    for copy in smalls:
        copy.start()

    zero_layer = jnp.zeros((ext, cols), jnp.float32)
    back_d[0] = jnp.zeros((8, cols), jnp.float32)

    field[2 + layer(slab)] = zero_layer

    @pl.when(jnp.logical_not(has_prev))
    def _():
        def clear(j, carry):
            field[j, pl.ds(rows + 6, 2), :] = jnp.zeros((2, cols), jnp.float32)
            return carry

        lax.fori_loop(0, slab + 4, clear, 0)

        def clear_back(j, carry):
            back_y[j, pl.ds(0, 2), :] = jnp.zeros((2, cols), jnp.float32)
            return carry

        lax.fori_loop(0, slab, clear_back, 0)

    @pl.when(jnp.logical_not(has_next))
    def _():
        def clear(j, carry):
            field[j, pl.ds(rows, 2), :] = jnp.zeros((2, cols), jnp.float32)
            return carry

        lax.fori_loop(0, slab + 4, clear, 0)

        def clear_back(j, carry):
            back_y[j, pl.ds(6, 2), :] = jnp.zeros((2, cols), jnp.float32)
            return carry

        lax.fori_loop(0, slab, clear_back, 0)

    barrier = pltpu.get_barrier_semaphore()
    pl.semaphore_signal(barrier, inc=1, device_id=across_id, device_id_type=MESH)

    @pl.when(has_prev)
    def _():
        pl.semaphore_signal(barrier, inc=1, device_id=prev_id, device_id_type=MESH)
        pl.semaphore_signal(barrier, inc=1, device_id=prev_across, device_id_type=MESH)

    @pl.when(has_next)
    def _():
        pl.semaphore_signal(barrier, inc=1, device_id=next_id, device_id_type=MESH)
        pl.semaphore_signal(barrier, inc=1, device_id=next_across, device_id_type=MESH)

    pl.semaphore_wait(barrier, 1 + 2 * has_prev.astype(jnp.int32) + 2 * has_next.astype(jnp.int32))

    face = pltpu.make_async_remote_copy(
        density.at[pl.ds(other * (slab - 2), 2)],
        field.at[pl.ds(core * (slab + 2), 2), pl.ds(0, rows), :],
        face_send.at[0], face_recv.at[0], device_id=across_id, device_id_type=MESH,
    )
    face_z = other * (slab - 1)
    face_at = 2 + core * slab - other
    corner_prev = pltpu.make_async_remote_copy(
        density.at[pl.ds(face_z, 1), pl.ds(0, 1), :],
        field.at[pl.ds(face_at, 1), pl.ds(rows, 1), :],
        face_send.at[1], face_recv.at[1], device_id=prev_across, device_id_type=MESH,
    )
    corner_next = pltpu.make_async_remote_copy(
        density.at[pl.ds(face_z, 1), pl.ds(rows - 1, 1), :],
        field.at[pl.ds(face_at, 1), pl.ds(rows + 7, 1), :],
        face_send.at[2], face_recv.at[2], device_id=next_across, device_id_type=MESH,
    )

    def halo_prev(i):
        start = chunk_start(i)
        return pltpu.make_async_remote_copy(
            density.at[pl.ds(start, step), pl.ds(0, 2), :],
            field.at[pl.ds(2 + start, step), pl.ds(rows, 2), :],
            halo_send.at[0, i], halo_recv.at[0, i], device_id=prev_id, device_id_type=MESH,
        )

    def halo_next(i):
        start = chunk_start(i)
        return pltpu.make_async_remote_copy(
            density.at[pl.ds(start, step), pl.ds(rows - 2, 2), :],
            field.at[pl.ds(2 + start, step), pl.ds(rows + 6, 2), :],
            halo_send.at[1, i], halo_recv.at[1, i], device_id=next_id, device_id_type=MESH,
        )

    face.start()

    @pl.when(has_prev)
    def _():
        corner_prev.start()

    @pl.when(has_next)
    def _():
        corner_next.start()

    for i in range(CHUNKS):

        @pl.when(has_prev)
        def _(i=i):
            halo_prev(i).start()

        @pl.when(has_next)
        def _(i=i):
            halo_next(i).start()

    for copy in smalls:
        copy.wait()
    row_of = lax.broadcasted_iota(jnp.int32, (rows, cols), 0)
    view = jnp.zeros((rows, cols), jnp.int32)
    for y in range(rows):
        view = jnp.where(row_of == y, view_s[y], view)
    ascending = view == other
    absorb = ab_v[...]
    half_light = [0.5 * light_s[0] * sign.astype(jnp.float32), 0.5 * light_s[1], 0.5 * light_s[2]]
    for c in range(3):
        table = jnp.broadcast_to(pal_v[pl.ds(c, 1), :], (8, pal_v.shape[1]))
        for y in range(0, rows, 8):
            for x in range(0, cols, 128):
                picked = jnp.take_along_axis(table, ids_v[pl.ds(y, 8), pl.ds(x, 128)], axis=1, mode="promise_in_bounds")
                tgt_v[c, pl.ds(y, 8), pl.ds(x, 128)] = picked

    own.wait()
    face.wait_recv()

    @pl.when(has_prev)
    def _():
        corner_next.wait_recv()

    @pl.when(has_next)
    def _():
        corner_prev.wait_recv()

    def blur(k):
        at = 2 + layer(k)
        here = field[at]
        total = 2.0 * here + field[at - 1] + field[at + 1]
        total = total + (ry(here, 1) + ry(here, -1)) + (rx(here, 1) + rx(here, -1))
        smooth[k + 1] = total

    scale = absorb * (LOG2E / depth_count)
    slope = absorb * (1.0 / (8.0 * depth_count))

    def shade(k, depth):
        here = smooth[k + 1]
        mid = here[:rows]
        dz = smooth[k + 2, pl.ds(0, rows), :] - smooth[k, pl.ds(0, rows), :]
        dy = ry(here, -1)[:rows] - ry(here, 1)[:rows]
        dx = rx(mid, -1) - rx(mid, 1)
        inv = lax.rsqrt(256.0 + dz * dz + dy * dy + dx * dx)
        facing = (half_light[0] * dz + half_light[1] * dy + half_light[2] * dx) * inv
        bend = facing * inv
        shade_b[k] = 0.5 + facing
        cz_b[k] = inv * (half_light[0] - bend * dz)
        cy_b[k] = inv * (half_light[1] - bend * dy)
        cx_b[k] = inv * (half_light[2] - bend * dx)
        power = mid * (LOG2E / 8.0)
        plus = jnp.log(1.0 + lax.exp2(power))
        fac_b[k] = slope * lax.exp2(power - plus * LOG2E)
        edge_b[k] = depth
        return depth + scale * plus

    def run(lo, count, unroll, one, carry):
        def several(j, carry):
            for u in range(unroll):
                carry = one(lo + j * unroll + u, carry)
            return carry

        return lax.fori_loop(0, count // unroll, several, carry)

    def blur_one(k, carry):
        blur(k)
        return carry

    depth = jnp.zeros((rows, cols), jnp.float32)
    for i in range(CHUNKS):

        @pl.when(has_prev)
        def _(i=i):
            halo_next(i).wait_recv()

        @pl.when(has_next)
        def _(i=i):
            halo_prev(i).wait_recv()

        run(step * i - 1, step, 8, blur_one, 0)
        if i:
            depth = run(step * (i - 1), step, 8, shade, depth)
    blur(slab - 1)
    smooth[slab + 1] = field[2 + layer(slab - 1)]
    depth = run(slab - step, step, 8, shade, depth)

    toward = jnp.where(ascending, -1.0, 1.0)
    base = jnp.where(ascending, 0.0, -depth)

    def composite(k, carry):
        left, m0, m1, m2, m3 = carry
        right = lax.exp2(toward * edge_b[k + 1] + base)
        mid = smooth[k + 1, pl.ds(0, rows), :]
        part = jnp.abs(left - right) * shade_b[k]
        m0 = m0 + part
        part = part * mid
        m1 = m1 + part
        part = part * mid
        m2 = m2 + part
        part = part * mid
        m3 = m3 + part
        edge_b[k] = left
        return (right, m0, m1, m2, m3)

    edge_b[slab] = depth
    zero = jnp.zeros((rows, cols), jnp.float32)
    left = lax.exp2(base)
    right, m0, m1, m2, m3 = run(0, slab, 8, composite, (left, zero, zero, zero, zero))
    edge_b[slab] = right
    for c in range(3):
        mine[c] = coef_s[c, 0] * m0 + (coef_s[c, 1] / 8.0) * m1 + (coef_s[c, 2] / 64.0) * m2 + (coef_s[c, 3] / 512.0) * m3
    mine[3] = depth
    swap = pltpu.make_async_remote_copy(
        mine, theirs, mid_send, mid_recv, device_id=across_id, device_id_type=MESH
    )
    swap.start()
    swap.wait()

    enter = jnp.where(ascending, lax.exp2(-theirs[3]), 1.0)
    leave = lax.exp2(-depth)
    misfit = []
    before = jnp.zeros((rows, cols), jnp.float32)
    for c in range(3):
        colour = jnp.where(ascending, theirs[c] + enter * mine[c], mine[c] + leave * theirs[c])
        image_v[c] = colour
        gap = (colour - tgt_v[c]) * float(depth_count)
        misfit.append(gap)
        before = before + gap * jnp.where(ascending, mine[c], theirs[c])
    rest = jnp.where(ascending, enter, leave) * before
    share = rows // 2
    image_copy = pltpu.make_async_copy(
        image_v.at[:, pl.ds(pl.multiple_of(core * share, 8), share), :], image_out, out_sem.at[CHUNKS]
    )
    image_copy.start()
    ramp = [
        enter
        * (misfit[0] * coef_s[0, i] + misfit[1] * coef_s[1, i] + misfit[2] * coef_s[2, i])
        * (1.0 / 8.0**i)
        for i in range(4)
    ]
    ramp2 = 2.0 * ramp[2]
    ramp3 = 3.0 * ramp[3]
    blank = jnp.zeros((8, cols), jnp.float32)

    def pull(k, rest):
        left = edge_b[k]
        signed = left - edge_b[k + 1]
        weight = jnp.abs(signed)
        mid = smooth[k + 1, pl.ds(0, rows), :]
        lit = shade_b[k]
        value = ramp[0] + mid * (ramp[1] + mid * (ramp[2] + mid * ramp[3]))
        deriv = ramp[1] + mid * (ramp2 + mid * ramp3)
        shown = lit * value
        pulled = weight * value
        direct = weight * lit * deriv + (left * shown - rest) * fac_b[k]
        qx = pulled * cx_b[k]
        qy = jnp.concatenate([pulled * cy_b[k], blank], 0)
        direct = direct + rx(qx, 1) - rx(qx, -1)
        ay_b[k] = ry(qy, 1) - ry(qy, -1) + jnp.concatenate([direct, blank], 0)
        qz_b[k + 1] = pulled * cz_b[k]
        return rest - signed * shown

    def gather(k, carry):
        full_b[k + 2, pl.ds(0, rows), :] = ay_b[k, pl.ds(0, rows), :] + qz_b[k] - qz_b[k + 2]
        full_b[k + 2, pl.ds(rows, 8), :] = ay_b[k, pl.ds(rows, 8), :]
        return carry

    def spread(k, carry):
        here = full_b[k + 2]
        total = 2.0 * here + full_b[k + 1] + full_b[k + 3]
        total = total + (ry(here, 1) + ry(here, -1)) + (rx(here, 1) + rx(here, -1))
        grad_b[2 + layer(k)] = total
        return carry

    def back_prev(i):
        start = chunk_start(i)
        return pltpu.make_async_remote_copy(
            grad_b.at[pl.ds(2 + start, step), pl.ds(rows + 6, 2), :],
            back_y.at[pl.ds(start, step), pl.ds(6, 2), :],
            ret_send.at[0, i], ret_recv.at[0, i], device_id=prev_id, device_id_type=MESH,
        )

    def back_next(i):
        start = chunk_start(i)
        return pltpu.make_async_remote_copy(
            grad_b.at[pl.ds(2 + start, step), pl.ds(rows, 2), :],
            back_y.at[pl.ds(start, step), pl.ds(0, 2), :],
            ret_send.at[1, i], ret_recv.at[1, i], device_id=next_id, device_id_type=MESH,
        )

    back_face = pltpu.make_async_remote_copy(
        grad_b.at[pl.ds(other * (slab + 2), 2), pl.ds(0, rows), :],
        back_z,
        face_send.at[3], face_recv.at[3], device_id=across_id, device_id_type=MESH,
    )
    back_corner_prev = pltpu.make_async_remote_copy(
        grad_b.at[face_ext(core, slab), pl.ds(rows + 7, 1), :],
        back_d.at[:, pl.ds(7, 1), :],
        face_send.at[4], face_recv.at[4], device_id=prev_across, device_id_type=MESH,
    )
    back_corner_next = pltpu.make_async_remote_copy(
        grad_b.at[face_ext(core, slab), pl.ds(rows, 1), :],
        back_d.at[:, pl.ds(0, 1), :],
        face_send.at[5], face_recv.at[5], device_id=next_across, device_id_type=MESH,
    )

    def send_back(i):
        @pl.when(has_prev)
        def _():
            back_prev(i).start()

        @pl.when(has_next)
        def _():
            back_next(i).start()

    qz_b[0] = zero
    qz_b[slab + 1] = zero
    for i in range(CHUNKS):
        rest = run(step * i, step, 8, pull, rest)
        if i == 0:
            full_b[0] = zero_layer
            full_b[1, pl.ds(0, rows), :] = -qz_b[1]
            full_b[1, pl.ds(rows, 8), :] = blank
            run(0, step - 1, 1, gather, 0)
            spread(-1, 0)
            grad_b[2 + layer(-2), pl.ds(0, rows), :] = full_b[1, pl.ds(0, rows), :]
            back_face.start()

            @pl.when(has_prev)
            def _():
                back_corner_prev.start()

            @pl.when(has_next)
            def _():
                back_corner_next.start()
        else:
            run(step * i - 1, step, 8, gather, 0)
            run(step * (i - 1), step, 8, spread, 0)
            send_back(i - 1)
    gather(slab - 1, 0)
    full_b[slab + 2, pl.ds(0, rows), :] = qz_b[slab]
    full_b[slab + 2, pl.ds(rows, 8), :] = blank
    run(slab - step, step, 8, spread, 0)
    send_back(CHUNKS - 1)

    row8 = lax.broadcasted_iota(jnp.int32, (8, cols), 0)

    def add(k, carry):
        z = layer(k)
        more = back_y[z]
        grad_b[2 + z, pl.ds(0, 8), :] = grad_b[2 + z, pl.ds(0, 8), :] + jnp.where(row8 < 2, more, 0.0)
        grad_b[2 + z, pl.ds(rows - 8, 8), :] = grad_b[2 + z, pl.ds(rows - 8, 8), :] + jnp.where(row8 > 5, more, 0.0)
        return carry

    outs = []
    for i in range(CHUNKS):
        start = chunk_start(i)
        if i == 0:
            back_face.wait_recv()

            @pl.when(has_prev)
            def _():
                back_corner_next.wait_recv()

            @pl.when(has_next)
            def _():
                back_corner_prev.wait_recv()

            near = 2 + layer(0)
            grad_b[near, pl.ds(0, rows), :] = grad_b[near, pl.ds(0, rows), :] + back_z[face_ext_in(core)]
            grad_b[near, pl.ds(0, 8), :] = grad_b[near, pl.ds(0, 8), :] + jnp.where(row8 < 1, back_d[0], 0.0)
            grad_b[near, pl.ds(rows - 8, 8), :] = grad_b[near, pl.ds(rows - 8, 8), :] + jnp.where(row8 > 6, back_d[0], 0.0)
            near = 2 + layer(1)
            grad_b[near, pl.ds(0, rows), :] = grad_b[near, pl.ds(0, rows), :] + back_z[1 - face_ext_in(core)]

        @pl.when(has_prev)
        def _(i=i):
            back_next(i).wait_recv()

        @pl.when(has_next)
        def _(i=i):
            back_prev(i).wait_recv()

        @pl.when(has_prev)
        def _(i=i):
            back_prev(i).wait_send()

        @pl.when(has_next)
        def _(i=i):
            back_next(i).wait_send()

        run(step * i, step, 8, add, 0)
        out = pltpu.make_async_copy(
            grad_b.at[pl.ds(2 + start, step), pl.ds(0, rows), :], grad_out.at[pl.ds(start, step)], out_sem.at[i]
        )
        out.start()
        outs.append(out)

    face.wait_send()
    back_face.wait_send()

    @pl.when(has_prev)
    def _():
        corner_prev.wait_send()
        back_corner_prev.wait_send()
        for i in range(CHUNKS):
            halo_prev(i).wait_send()

    @pl.when(has_next)
    def _():
        corner_next.wait_send()
        back_corner_next.wait_send()
        for i in range(CHUNKS):
            halo_next(i).wait_send()

    image_copy.wait()
    for out in outs:
        out.wait()


def face_ext(core, slab):
    return pl.ds(core * 1 + (1 - core) * (slab + 2), 1)


def face_ext_in(core):
    return 1 - core


def solution(mesh):
    tiles = mesh.shape["tile"]

    def shards(density, absorption, view_dir, target_ids, palette, coef, light):
        slab, rows, cols = density.shape
        ext = rows + 8
        f32 = jnp.float32
        kernel = functools.partial(body, tiles, slab, rows, cols, 2 * slab)
        scratch = [
            pltpu.VMEM((slab + 4, ext, cols), f32),
            pltpu.VMEM((slab + 2, ext, cols), f32),
            *[pltpu.VMEM((slab, rows, cols), f32)] * 5,
            pltpu.VMEM((slab + 1, rows, cols), f32),
            pltpu.VMEM((slab, ext, cols), f32),
            pltpu.VMEM((slab + 2, rows, cols), f32),
            pltpu.VMEM((slab + 3, ext, cols), f32),
            pltpu.VMEM((slab + 4, ext, cols), f32),
            pltpu.VMEM(absorption.shape, f32),
            pltpu.VMEM(target_ids.shape, jnp.int32),
            pltpu.VMEM(palette.shape, f32),
            pltpu.SMEM(view_dir.shape, jnp.int32),
            pltpu.SMEM(coef.shape, f32),
            pltpu.SMEM(light.shape, f32),
            pltpu.VMEM((3, rows, cols), f32),
            pltpu.VMEM((4, rows, cols), f32),
            pltpu.VMEM((4, rows, cols), f32),
            pltpu.VMEM((3, rows, cols), f32),
            pltpu.VMEM((slab, 8, cols), f32),
            pltpu.VMEM((2, rows, cols), f32),
            pltpu.VMEM((1, 8, cols), f32),
            pltpu.SemaphoreType.DMA,
            pltpu.SemaphoreType.DMA((6,)),
            pltpu.SemaphoreType.DMA((2, CHUNKS)),
            pltpu.SemaphoreType.DMA((2, CHUNKS)),
            pltpu.SemaphoreType.DMA((6,)),
            pltpu.SemaphoreType.DMA((6,)),
            pltpu.SemaphoreType.DMA,
            pltpu.SemaphoreType.DMA,
            pltpu.SemaphoreType.DMA((2, CHUNKS)),
            pltpu.SemaphoreType.DMA((2, CHUNKS)),
            pltpu.SemaphoreType.DMA((CHUNKS + 1,)),
        ]
        return pl.pallas_call(
            kernel,
            out_shape=(
                jax.ShapeDtypeStruct((3, rows // 2, cols), f32),
                jax.ShapeDtypeStruct(density.shape, f32),
            ),
            in_specs=[pl.BlockSpec(memory_space=pl.ANY)] * 7,
            out_specs=[pl.BlockSpec(memory_space=pl.ANY)] * 2,
            scratch_shapes=scratch,
            compiler_params=pltpu.CompilerParams(
                collective_id=0, has_side_effects=True, vmem_limit_bytes=24 * 1024 * 1024
            ),
            cost_estimate=pl.CostEstimate(flops=200 * slab * rows * cols, bytes_accessed=8 * slab * rows * cols, transcendentals=0),
        )(*[pltpu.with_memory_space_constraint(x, pltpu.HBM) for x in (density, absorption, view_dir, target_ids, palette, coef, light)])

    placed = (P("depth", "tile", None), P("tile", None), P("tile"), P("tile", None), P(), P(), P())
    return jax.shard_map(
        shards,
        mesh=mesh,
        in_specs=placed,
        out_specs=(P(None, ("tile", "depth"), None), P("depth", "tile", None)),
        check_vma=False,
    )
```

```python
import functools
import math

import jax
import jax.numpy as jnp
from jax import lax
from jax.experimental import pallas as pl
from jax.experimental.pallas import tpu as pltpu
from jax.sharding import PartitionSpec as P

MESH = pl.DeviceIdType.MESH
LOG2E = math.log2(math.e)
CHUNKS = 4


def body(
    tiles, slab, rows, cols, depth_count,
    density, absorption, view_dir, target_ids, palette, coef, light,
    image_v, grad_b, back_y,
    field, smooth, shade_b, cz_b, cy_b, cx_b, fac_b, edge_b, ay_b, qz_b, full_b,
    ab_v, ids_v, pal_v, view_s, coef_s, light_s, mine, theirs, tgt_v, back_z, colours,
    load_sem, small_sem, halo_send, halo_recv, core_send, core_recv, ret_send, ret_recv,
):
    tile = lax.axis_index("tile")
    core = lax.axis_index("depth")
    other = 1 - core
    has_prev = tile > 0
    has_next = tile < tiles - 1
    ext = rows + 8
    step = slab // CHUNKS
    sign = 2 * core - 1
    first = (1 - core) * (slab - 1)

    def layer(k):
        return first + sign * k

    def chunk_start(i):
        return core * (step * i) + other * (slab - step - step * i)

    prev_id = (jnp.maximum(tile - 1, 0), core)
    next_id = (jnp.minimum(tile + 1, tiles - 1), core)
    across_id = (tile, other)

    def rx(value, shift):
        return pltpu.roll(value, shift % cols, 1)

    def ry(value, shift):
        return pltpu.roll(value, shift % ext, 0)

    barrier = pltpu.get_barrier_semaphore()
    pl.semaphore_signal(barrier, inc=1, device_id=across_id, device_id_type=MESH)

    @pl.when(has_prev)
    def _():
        pl.semaphore_signal(barrier, inc=1, device_id=prev_id, device_id_type=MESH)

    @pl.when(has_next)
    def _():
        pl.semaphore_signal(barrier, inc=1, device_id=next_id, device_id_type=MESH)

    own = pltpu.make_async_copy(density, field.at[pl.ds(2, slab), pl.ds(0, rows), :], load_sem)
    own.start()
    smalls = [
        pltpu.make_async_copy(src, dst, small_sem.at[n])
        for n, (src, dst) in enumerate(
            [(view_dir, view_s), (absorption, ab_v), (light, light_s), (coef, coef_s), (target_ids, ids_v), (palette, pal_v)]
        )
    ]
    for copy in smalls:
        copy.start()

    zero_layer = jnp.zeros((ext, cols), jnp.float32)
    field[2 + layer(slab)] = zero_layer

    def clear_rows(at_field, at_back):
        def clear(j, carry):
            field[2 + j, pl.ds(at_field, 2), :] = jnp.zeros((2, cols), jnp.float32)
            back_y[j, pl.ds(at_back, 2), :] = jnp.zeros((2, cols), jnp.float32)
            return carry

        lax.fori_loop(0, slab, clear, 0)

    @pl.when(jnp.logical_not(has_prev))
    def _():
        clear_rows(rows + 6, 0)

    @pl.when(jnp.logical_not(has_next))
    def _():
        clear_rows(rows, 6)

    pl.semaphore_wait(barrier, 1 + has_prev.astype(jnp.int32) + has_next.astype(jnp.int32))

    def across(src, dst, n):
        return pltpu.make_async_remote_copy(
            src, dst, core_send.at[n], core_recv.at[n], device_id=across_id, device_id_type=MESH
        )

    face = across(
        density.at[pl.ds(other * (slab - 2), 2)], field.at[pl.ds(core * (slab + 2), 2), pl.ds(0, rows), :], 0
    )
    corner = across(
        field.at[pl.ds(2 + other * (slab - 1), 1), pl.ds(rows, 8), :],
        field.at[pl.ds(2 + core * slab - other, 1), pl.ds(rows, 8), :],
        1,
    )

    def halo_prev(i):
        start = chunk_start(i)
        return pltpu.make_async_remote_copy(
            density.at[pl.ds(start, step), pl.ds(0, 2), :],
            field.at[pl.ds(2 + start, step), pl.ds(rows, 2), :],
            halo_send.at[0, i], halo_recv.at[0, i], device_id=prev_id, device_id_type=MESH,
        )

    def halo_next(i):
        start = chunk_start(i)
        return pltpu.make_async_remote_copy(
            density.at[pl.ds(start, step), pl.ds(rows - 2, 2), :],
            field.at[pl.ds(2 + start, step), pl.ds(rows + 6, 2), :],
            halo_send.at[1, i], halo_recv.at[1, i], device_id=next_id, device_id_type=MESH,
        )

    for i in range(CHUNKS):

        @pl.when(has_prev)
        def _(i=i):
            halo_prev(i).start()

        @pl.when(has_next)
        def _(i=i):
            halo_next(i).start()

        if i == 0:
            face.start()

    def halo_arrived(i):
        @pl.when(has_prev)
        def _():
            halo_next(i).wait_recv()

        @pl.when(has_next)
        def _():
            halo_prev(i).wait_recv()

    for copy in smalls:
        copy.wait()
    row_of = lax.broadcasted_iota(jnp.int32, (rows, cols), 0)
    view = jnp.zeros((rows, cols), jnp.int32)
    for y in range(rows):
        view = jnp.where(row_of == y, view_s[y], view)
    ascending = view == other
    absorb = ab_v[...]
    half_light = [0.5 * light_s[0] * sign.astype(jnp.float32), 0.5 * light_s[1], 0.5 * light_s[2]]
    for c in range(3):
        table = jnp.broadcast_to(pal_v[pl.ds(c, 1), :], (8, pal_v.shape[1]))
        for y in range(0, rows, 8):
            for x in range(0, cols, 128):
                picked = jnp.take_along_axis(table, ids_v[pl.ds(y, 8), pl.ds(x, 128)], axis=1, mode="promise_in_bounds")
                tgt_v[c, pl.ds(y, 8), pl.ds(x, 128)] = picked

    own.wait()
    face.wait_recv()
    halo_arrived(0)
    corner.start()

    def blur(k):
        at = 2 + layer(k)
        here = field[at]
        total = 2.0 * here + field[at - 1] + field[at + 1]
        total = total + (ry(here, 1) + ry(here, -1)) + (rx(here, 1) + rx(here, -1))
        smooth[k + 1] = total

    scale = absorb * (LOG2E / depth_count)
    slope = absorb * (1.0 / (8.0 * depth_count))

    def shade(k, depth):
        here = smooth[k + 1]
        mid = here[:rows]
        dz = smooth[k + 2, pl.ds(0, rows), :] - smooth[k, pl.ds(0, rows), :]
        dy = ry(here, -1)[:rows] - ry(here, 1)[:rows]
        dx = rx(mid, -1) - rx(mid, 1)
        inv = lax.rsqrt(256.0 + dz * dz + dy * dy + dx * dx)
        facing = (half_light[0] * dz + half_light[1] * dy + half_light[2] * dx) * inv
        bend = facing * inv
        shade_b[k] = 0.5 + facing
        cz_b[k] = inv * (half_light[0] - bend * dz)
        cy_b[k] = inv * (half_light[1] - bend * dy)
        cx_b[k] = inv * (half_light[2] - bend * dx)
        power = mid * (LOG2E / 8.0)
        plus = jnp.log(1.0 + lax.exp2(power))
        fac_b[k] = slope * lax.exp2(power - plus * LOG2E)
        edge_b[k] = depth
        return depth + scale * plus

    def run(lo, count, unroll, one, carry):
        def several(j, carry):
            for u in range(unroll):
                carry = one(lo + j * unroll + u, carry)
            return carry

        return lax.fori_loop(0, count // unroll, several, carry)

    def blur_one(k, carry):
        blur(k)
        return carry

    zero = jnp.zeros((rows, cols), jnp.float32)
    tail = zero
    halo_arrived(1)
    run(1, 2 * step - 2, step - 1, blur_one, 0)
    tail = run(2, 2 * step - 4, step - 2, shade, tail)
    for i in range(2, CHUNKS - 1):
        halo_arrived(i)
        run(step * i - 1, step, step, blur_one, 0)
        tail = run(step * i - 2, step, step, shade, tail)
    halo_arrived(CHUNKS - 1)
    run(slab - step - 1, step + 1, step + 1, blur_one, 0)
    smooth[slab + 1] = field[2 + layer(slab - 1)]
    tail = run(slab - step - 2, step + 2, step + 2, shade, tail)
    corner.wait_recv()
    run(-1, 2, 2, blur_one, 0)
    depth0 = shade(0, zero)
    depth1 = shade(1, depth0)
    edge_b[0] = -depth1
    edge_b[1] = depth0 - depth1
    edge_b[slab] = tail
    depth = tail + depth1

    toward = jnp.where(ascending, -1.0, 1.0)
    base = jnp.where(ascending, -depth1, depth1 - depth)

    def composite(k, carry):
        left, m0, m1, m2, m3 = carry
        right = lax.exp2(toward * edge_b[k + 1] + base)
        mid = smooth[k + 1, pl.ds(0, rows), :]
        part = jnp.abs(left - right) * shade_b[k]
        m0 = m0 + part
        part = part * mid
        m1 = m1 + part
        part = part * mid
        m2 = m2 + part
        part = part * mid
        m3 = m3 + part
        edge_b[k] = left
        return (right, m0, m1, m2, m3)

    left = lax.exp2(base - toward * depth1)
    right, m0, m1, m2, m3 = run(0, slab, 8, composite, (left, zero, zero, zero, zero))
    edge_b[slab] = right
    for c in range(3):
        mine[c] = coef_s[c, 0] * m0 + (coef_s[c, 1] / 8.0) * m1 + (coef_s[c, 2] / 64.0) * m2 + (coef_s[c, 3] / 512.0) * m3
    mine[3] = depth
    swap = across(mine, theirs, 2)
    swap.start()
    swap.wait_recv()

    enter = jnp.where(ascending, lax.exp2(-theirs[3]), 1.0)
    leave = lax.exp2(-depth)
    misfit = []
    before = jnp.zeros((rows, cols), jnp.float32)
    for c in range(3):
        colour = jnp.where(ascending, theirs[c] + enter * mine[c], mine[c] + leave * theirs[c])
        colours[c] = colour
        gap = (colour - tgt_v[c]) * float(depth_count)
        misfit.append(gap)
        before = before + gap * jnp.where(ascending, mine[c], theirs[c])
    rest = jnp.where(ascending, enter, leave) * before
    share = rows // 2
    mine_rows = pl.ds(pl.multiple_of(core * share, 8), share)
    for c in range(3):
        image_v[c] = colours[c, mine_rows, :]
    ramp = [
        enter
        * (misfit[0] * coef_s[0, i] + misfit[1] * coef_s[1, i] + misfit[2] * coef_s[2, i])
        * (1.0 / 8.0**i)
        for i in range(4)
    ]
    ramp2 = 2.0 * ramp[2]
    ramp3 = 3.0 * ramp[3]
    blank = jnp.zeros((8, cols), jnp.float32)

    def pull(k, rest):
        left = edge_b[k]
        signed = left - edge_b[k + 1]
        weight = jnp.abs(signed)
        mid = smooth[k + 1, pl.ds(0, rows), :]
        lit = shade_b[k]
        value = ramp[0] + mid * (ramp[1] + mid * (ramp[2] + mid * ramp[3]))
        deriv = ramp[1] + mid * (ramp2 + mid * ramp3)
        shown = lit * value
        pulled = weight * value
        direct = weight * lit * deriv + (left * shown - rest) * fac_b[k]
        qx = pulled * cx_b[k]
        qy = jnp.concatenate([pulled * cy_b[k], blank], 0)
        direct = direct + rx(qx, 1) - rx(qx, -1)
        ay_b[k] = ry(qy, 1) - ry(qy, -1) + jnp.concatenate([direct, blank], 0)
        qz_b[k + 1] = pulled * cz_b[k]
        return rest - signed * shown

    def gather(k, carry):
        full_b[k + 2, pl.ds(0, rows), :] = ay_b[k, pl.ds(0, rows), :] + qz_b[k] - qz_b[k + 2]
        full_b[k + 2, pl.ds(rows, 8), :] = ay_b[k, pl.ds(rows, 8), :]
        return carry

    def spread(k, carry):
        here = full_b[k + 2]
        total = 2.0 * here + full_b[k + 1] + full_b[k + 3]
        total = total + (ry(here, 1) + ry(here, -1)) + (rx(here, 1) + rx(here, -1))
        grad_b[2 + layer(k)] = total
        return carry

    def back_prev(i):
        start = chunk_start(i)
        return pltpu.make_async_remote_copy(
            grad_b.at[pl.ds(2 + start, step), pl.ds(rows + 6, 2), :],
            back_y.at[pl.ds(start, step), pl.ds(6, 2), :],
            ret_send.at[0, i], ret_recv.at[0, i], device_id=prev_id, device_id_type=MESH,
        )

    def back_next(i):
        start = chunk_start(i)
        return pltpu.make_async_remote_copy(
            grad_b.at[pl.ds(2 + start, step), pl.ds(rows, 2), :],
            back_y.at[pl.ds(start, step), pl.ds(0, 2), :],
            ret_send.at[1, i], ret_recv.at[1, i], device_id=next_id, device_id_type=MESH,
        )

    back_face = across(grad_b.at[pl.ds(other * (slab + 2), 2)], back_z, 3)

    def send_back(i):
        @pl.when(has_prev)
        def _():
            back_prev(i).start()

        @pl.when(has_next)
        def _():
            back_next(i).start()

    qz_b[0] = zero
    qz_b[slab + 1] = zero
    rest = run(0, 2, 2, pull, rest)
    full_b[0] = zero_layer
    full_b[1, pl.ds(0, rows), :] = -qz_b[1]
    full_b[1, pl.ds(rows, 8), :] = blank
    gather(0, 0)
    spread(-1, 0)
    grad_b[2 + layer(-2)] = full_b[1]
    back_face.start()
    for i in range(CHUNKS - 1):
        rest = run(step * i + 2, step, step, pull, rest)
        run(step * i + 1, step, step, gather, 0)
        run(step * i, step, step, spread, 0)
        if i:
            send_back(i)
    run(slab - step + 2, step - 2, step - 2, pull, rest)
    run(slab - step + 1, step - 1, step - 1, gather, 0)
    full_b[slab + 2, pl.ds(0, rows), :] = qz_b[slab]
    full_b[slab + 2, pl.ds(rows, 8), :] = blank
    run(slab - step, step, step, spread, 0)
    send_back(CHUNKS - 1)

    back_face.wait_recv()
    near = 2 + layer(0)
    grad_b[near] = grad_b[near] + back_z[other]
    near = 2 + layer(1)
    grad_b[near] = grad_b[near] + back_z[core]
    send_back(0)

    face.wait_send()
    corner.wait_send()
    swap.wait_send()
    back_face.wait_send()

    @pl.when(has_prev)
    def _():
        for i in range(CHUNKS):
            halo_prev(i).wait_send()

    @pl.when(has_next)
    def _():
        for i in range(CHUNKS):
            halo_next(i).wait_send()

    for i in (*range(1, CHUNKS), 0):

        @pl.when(has_prev)
        def _(i=i):
            back_prev(i).wait_send()
            back_next(i).wait_recv()

        @pl.when(has_next)
        def _(i=i):
            back_next(i).wait_send()
            back_prev(i).wait_recv()


def finish(image_v, grad_b, back_y, image_out, grad_out, total, sems):
    slab, rows, cols = total.shape
    step = slab // CHUNKS
    image_copy = pltpu.make_async_copy(image_v, image_out, sems.at[CHUNKS])
    image_copy.start()
    row8 = lax.broadcasted_iota(jnp.int32, (8, cols), 0)
    outs = []
    for i in range(CHUNKS):
        for z in range(step * i, step * i + step):
            more = back_y[z]
            total[z, pl.ds(0, 8), :] = grad_b[2 + z, pl.ds(0, 8), :] + jnp.where(row8 < 2, more, 0.0)
            total[z, pl.ds(rows - 8, 8), :] = grad_b[2 + z, pl.ds(rows - 8, 8), :] + jnp.where(row8 > 5, more, 0.0)
        out = pltpu.make_async_copy(total.at[pl.ds(step * i, step)], grad_out.at[pl.ds(step * i, step)], sems.at[i])
        out.start()
        outs.append(out)
    image_copy.wait()
    for out in outs:
        out.wait()


def solution(mesh):
    tiles = mesh.shape["tile"]

    def shards(density, absorption, view_dir, target_ids, palette, coef, light):
        slab, rows, cols = density.shape
        ext = rows + 8
        f32 = jnp.float32
        kernel = functools.partial(body, tiles, slab, rows, cols, 2 * slab)
        scratch = [
            pltpu.VMEM((slab + 4, ext, cols), f32),
            pltpu.VMEM((slab + 2, ext, cols), f32),
            *[pltpu.VMEM((slab, rows, cols), f32)] * 5,
            pltpu.VMEM((slab + 1, rows, cols), f32),
            pltpu.VMEM((slab, ext, cols), f32),
            pltpu.VMEM((slab + 2, rows, cols), f32),
            pltpu.VMEM((slab + 3, ext, cols), f32),
            pltpu.VMEM(absorption.shape, f32),
            pltpu.VMEM(target_ids.shape, jnp.int32),
            pltpu.VMEM(palette.shape, f32),
            pltpu.SMEM(view_dir.shape, jnp.int32),
            pltpu.SMEM(coef.shape, f32),
            pltpu.SMEM(light.shape, f32),
            pltpu.VMEM((4, rows, cols), f32),
            pltpu.VMEM((4, rows, cols), f32),
            pltpu.VMEM((3, rows, cols), f32),
            pltpu.VMEM((2, ext, cols), f32),
            pltpu.VMEM((3, rows, cols), f32),
            pltpu.SemaphoreType.DMA,
            pltpu.SemaphoreType.DMA((6,)),
            pltpu.SemaphoreType.DMA((2, CHUNKS)),
            pltpu.SemaphoreType.DMA((2, CHUNKS)),
            pltpu.SemaphoreType.DMA((4,)),
            pltpu.SemaphoreType.DMA((4,)),
            pltpu.SemaphoreType.DMA((2, CHUNKS)),
            pltpu.SemaphoreType.DMA((2, CHUNKS)),
        ]
        image, grad, back = pl.pallas_call(
            kernel,
            out_shape=(
                pltpu.VMEM((3, rows // 2, cols), f32),
                pltpu.VMEM((slab + 4, ext, cols), f32),
                pltpu.VMEM((slab, 8, cols), f32),
            ),
            in_specs=[pl.BlockSpec(memory_space=pl.ANY)] * 7,
            out_specs=[pl.BlockSpec(memory_space=pltpu.VMEM)] * 3,
            scratch_shapes=scratch,
            compiler_params=pltpu.CompilerParams(
                collective_id=0, has_side_effects=True, vmem_limit_bytes=24 * 1024 * 1024
            ),
            cost_estimate=pl.CostEstimate(flops=200 * slab * rows * cols, bytes_accessed=8 * slab * rows * cols, transcendentals=0),
        )(*[pltpu.with_memory_space_constraint(x, pltpu.HBM) for x in (density, absorption, view_dir, target_ids, palette, coef, light)])
        return pl.pallas_call(
            finish,
            out_shape=(jax.ShapeDtypeStruct(image.shape, f32), jax.ShapeDtypeStruct(density.shape, f32)),
            in_specs=[pl.BlockSpec(memory_space=pltpu.VMEM)] * 3,
            out_specs=[pl.BlockSpec(memory_space=pl.ANY)] * 2,
            scratch_shapes=[pltpu.VMEM(density.shape, f32), pltpu.SemaphoreType.DMA((CHUNKS + 1,))],
            compiler_params=pltpu.CompilerParams(vmem_limit_bytes=8 * 1024 * 1024),
        )(image, grad, back)

    placed = (P("depth", "tile", None), P("tile", None), P("tile"), P("tile", None), P(), P(), P())
    return jax.shard_map(
        shards,
        mesh=mesh,
        in_specs=placed,
        out_specs=(P(None, ("tile", "depth"), None), P("depth", "tile", None)),
        check_vma=False,
    )
```

```python
import functools
import math

import jax
import jax.numpy as jnp
from jax import lax
from jax.experimental import pallas as pl
from jax.experimental.pallas import tpu as pltpu
from jax.sharding import PartitionSpec as P

MESH = pl.DeviceIdType.MESH
LOG2E = math.log2(math.e)
CHUNKS = 4
HALO = 4


def run(lo, count, unroll, one, carry):
    def several(j, carry):
        for u in range(unroll):
            carry = one(lo + j * unroll + u, carry)
        return carry

    return lax.fori_loop(0, count // unroll, several, carry)


def forward(
    tiles, slab, rows, cols, depth_count,
    density, absorption, view_dir, target_ids, palette, coef, light,
    smooth, shade_b, cz_b, cy_b, cx_b, fac_b, edge_b, ramp_b, image_v,
    field, info, plus_b, inv_b, ids_v, pal_v, view_s, coef_s, light_s, mine, theirs, colours,
    load_sem, small_sem, halo_send, halo_recv, core_send, core_recv,
):
    tile = lax.axis_index("tile")
    core = lax.axis_index("depth")
    other = 1 - core
    has_prev = tile > 0
    has_next = tile < tiles - 1
    ext = rows + 2 * HALO
    step = slab // CHUNKS
    sign = 2 * core - 1
    first = (1 - core) * (slab - 1)

    def layer(k):
        return first + sign * k

    def chunk_start(i):
        return core * (step * i) + other * (slab - step - step * i)

    prev_id = (jnp.maximum(tile - 1, 0), core)
    next_id = (jnp.minimum(tile + 1, tiles - 1), core)
    across_id = (tile, other)

    def rx(value, shift):
        return pltpu.roll(value, shift % cols, 1)

    def ry(value, shift):
        return pltpu.roll(value, shift % ext, 0)

    barrier = pltpu.get_barrier_semaphore()
    pl.semaphore_signal(barrier, inc=1, device_id=across_id, device_id_type=MESH)

    @pl.when(has_prev)
    def _():
        pl.semaphore_signal(barrier, inc=1, device_id=prev_id, device_id_type=MESH)

    @pl.when(has_next)
    def _():
        pl.semaphore_signal(barrier, inc=1, device_id=next_id, device_id_type=MESH)

    own = pltpu.make_async_copy(density, field.at[pl.ds(HALO, slab), pl.ds(0, rows), :], load_sem)
    smalls = [
        pltpu.make_async_copy(src, dst, small_sem.at[n])
        for n, (src, dst) in enumerate(
            [
                (view_dir, view_s),
                (absorption, info.at[0, pl.ds(0, rows), :]),
                (light, light_s),
                (coef, coef_s),
                (target_ids, ids_v),
                (palette, pal_v),
            ]
        )
    ]
    for copy in smalls:
        copy.start()
    own.start()

    field[HALO + layer(slab)] = jnp.zeros((ext, cols), jnp.float32)

    def clear_rows(at):
        def clear(j, carry):
            field[HALO + j, pl.ds(at, HALO), :] = jnp.zeros((HALO, cols), jnp.float32)
            return carry

        lax.fori_loop(0, slab, clear, 0)
        for n in range(5):
            info[n, pl.ds(at, HALO), :] = jnp.zeros((HALO, cols), jnp.float32)

    @pl.when(jnp.logical_not(has_prev))
    def _():
        clear_rows(rows + HALO)

    @pl.when(jnp.logical_not(has_next))
    def _():
        clear_rows(rows)

    pl.semaphore_wait(barrier, 1 + has_prev.astype(jnp.int32) + has_next.astype(jnp.int32))

    def across(src, dst, n):
        return pltpu.make_async_remote_copy(
            src, dst, core_send.at[n], core_recv.at[n], device_id=across_id, device_id_type=MESH
        )

    face_at = core * (slab + HALO)
    face = across(
        density.at[pl.ds(other * (slab - HALO), HALO)], field.at[pl.ds(face_at, HALO), pl.ds(0, rows), :], 0
    )
    corner = across(
        field.at[pl.ds(HALO + other * (slab - HALO), HALO), pl.ds(rows, 2 * HALO), :],
        field.at[pl.ds(face_at, HALO), pl.ds(rows, 2 * HALO), :],
        1,
    )

    def to_prev(src, dst, n):
        return pltpu.make_async_remote_copy(
            src, dst, halo_send.at[0, n], halo_recv.at[0, n], device_id=prev_id, device_id_type=MESH
        )

    def to_next(src, dst, n):
        return pltpu.make_async_remote_copy(
            src, dst, halo_send.at[1, n], halo_recv.at[1, n], device_id=next_id, device_id_type=MESH
        )

    low, high = pl.ds(0, HALO), pl.ds(rows - HALO, HALO)
    after, before_rows = pl.ds(rows, HALO), pl.ds(rows + HALO, HALO)

    def halo_prev(i):
        if i == CHUNKS:
            return to_prev(info.at[:, low, :], info.at[:, after, :], i)
        start = chunk_start(i)
        return to_prev(density.at[pl.ds(start, step), low, :], field.at[pl.ds(HALO + start, step), after, :], i)

    def halo_next(i):
        if i == CHUNKS:
            return to_next(info.at[:, high, :], info.at[:, before_rows, :], i)
        start = chunk_start(i)
        return to_next(density.at[pl.ds(start, step), high, :], field.at[pl.ds(HALO + start, step), before_rows, :], i)

    def halo_start(i):
        @pl.when(has_prev)
        def _():
            halo_prev(i).start()

        @pl.when(has_next)
        def _():
            halo_next(i).start()

    def halo_arrived(i):
        @pl.when(has_prev)
        def _():
            halo_next(i).wait_recv()

        @pl.when(has_next)
        def _():
            halo_prev(i).wait_recv()

    halo_start(0)
    face.start()
    for i in range(1, CHUNKS):
        halo_start(i)

    for copy in smalls:
        copy.wait()
    own_row = lax.broadcasted_iota(jnp.int32, (rows, cols), 0)
    view = jnp.zeros((rows, cols), jnp.int32)
    for y in range(rows):
        view = jnp.where(own_row == y, view_s[y], view)
    info[1, pl.ds(0, rows), :] = view.astype(jnp.float32)
    for c in range(3):
        table = jnp.broadcast_to(pal_v[pl.ds(c, 1), :], (8, pal_v.shape[1]))
        for y in range(0, rows, 8):
            for x in range(0, cols, 128):
                picked = jnp.take_along_axis(table, ids_v[pl.ds(y, 8), pl.ds(x, 128)], axis=1, mode="promise_in_bounds")
                info[2 + c, pl.ds(y, 8), pl.ds(x, 128)] = picked
    halo_start(CHUNKS)
    half_light = [0.5 * light_s[0] * sign.astype(jnp.float32), 0.5 * light_s[1], 0.5 * light_s[2]]

    own.wait()
    halo_arrived(0)
    corner.start()
    halo_arrived(CHUNKS)
    absorb = info[0]
    ascending = info[1] == other.astype(jnp.float32)
    scale = absorb * (LOG2E / depth_count)
    slope = absorb * (1.0 / (8.0 * depth_count))

    def blur(k, carry):
        at = HALO + layer(k)
        here = field[at]
        total = 2.0 * here + field[at - 1] + field[at + 1]
        total = total + (ry(here, 1) + ry(here, -1)) + (rx(here, 1) + rx(here, -1))
        smooth[k + 3] = total
        return carry

    def shade(k):
        here = smooth[k + 3]
        dz = smooth[k + 4] - smooth[k + 2]
        dy = ry(here, -1) - ry(here, 1)
        dx = rx(here, -1) - rx(here, 1)
        inv = lax.rsqrt(256.0 + dz * dz + dy * dy + dx * dx)
        facing = (half_light[0] * dz + half_light[1] * dy + half_light[2] * dx) * inv
        shade_b[k + 2] = 0.5 + facing
        cz_b[k + 2] = dz
        cy_b[k + 2] = dy
        cx_b[k + 2] = dx
        inv_b[k + 2] = inv
        plus = jnp.log(1.0 + lax.exp2(here * (LOG2E / 8.0)))
        plus_b[k + 2] = plus
        return scale * plus

    def shade_up(k, depth):
        edge_b[k + 2] = depth
        return depth + shade(k)

    def shade_down(j, depth):
        k = -j
        depth = depth - shade(k)
        edge_b[k + 2] = depth
        return depth

    zero = jnp.zeros((ext, cols), jnp.float32)
    halo_arrived(1)
    run(1, 2 * step - 2, step - 1, blur, 0)
    far = run(2, 2 * step - 4, step - 2, shade_up, zero)
    for i in range(2, CHUNKS - 1):
        halo_arrived(i)
        run(step * i - 1, step, step, blur, 0)
        far = run(step * i - 2, step, step, shade_up, far)
    face.wait_recv()
    corner.wait_recv()
    run(-3, 4, 4, blur, 0)
    near = run(-1, 2, 2, shade_down, zero)
    run(1, 2, 2, shade_down, near)
    halo_arrived(CHUNKS - 1)
    run(slab - step - 1, step + 1, step + 1, blur, 0)
    smooth[slab + 3] = field[HALO + layer(slab - 1)]
    far = run(slab - step - 2, step + 2, step + 2, shade_up, far)

    toward = jnp.where(ascending, -1.0, 1.0)
    base = jnp.where(ascending, near, -far)
    depth = far - near

    def light_at(k):
        return lax.exp2(toward * edge_b[k + 2] + base)

    def composite(k, carry):
        left, m0, m1, m2, m3 = carry
        right = light_at(k + 1)
        here = smooth[k + 3]
        part = jnp.abs(left - right) * shade_b[k + 2]
        m0 = m0 + part
        part = part * here
        m1 = m1 + part
        part = part * here
        m2 = m2 + part
        part = part * here
        m3 = m3 + part
        edge_b[k + 2] = left
        return (right, m0, m1, m2, m3)

    edge_b[slab + 2] = far
    right, m0, m1, m2, m3 = run(0, slab, 8, composite, (light_at(0), zero, zero, zero, zero))
    edge_b[slab + 2] = right
    for c in range(3):
        mine[c] = coef_s[c, 0] * m0 + (coef_s[c, 1] / 8.0) * m1 + (coef_s[c, 2] / 64.0) * m2 + (coef_s[c, 3] / 512.0) * m3
    mine[3] = depth
    swap = across(mine, theirs, 2)
    swap.start()

    edge_b[0] = light_at(-2)
    edge_b[1] = light_at(-1)

    def bend(k, carry):
        inv = inv_b[k + 2]
        turn = (shade_b[k + 2] - 0.5) * inv
        cz_b[k + 2] = inv * (half_light[0] - turn * cz_b[k + 2])
        cy_b[k + 2] = inv * (half_light[1] - turn * cy_b[k + 2])
        cx_b[k + 2] = inv * (half_light[2] - turn * cx_b[k + 2])
        fac_b[k + 2] = slope * lax.exp2(smooth[k + 3] * (LOG2E / 8.0) - plus_b[k + 2] * LOG2E)
        return carry

    run(-2, slab, 8, bend, 0)
    run(slab - 2, 2, 2, bend, 0)
    enter0 = lax.exp2(-depth)
    swap.wait_recv()

    enter = jnp.where(ascending, lax.exp2(-theirs[3]), 1.0)
    row = lax.broadcasted_iota(jnp.int32, (ext, cols), 0)
    present = jnp.where(row < rows, 1.0, jnp.where(row < rows + HALO, has_next.astype(jnp.float32), has_prev.astype(jnp.float32)))
    present = present * float(depth_count)
    misfit = []
    before = zero
    for c in range(3):
        colour = jnp.where(ascending, theirs[c] + enter * mine[c], mine[c] + enter0 * theirs[c])
        colours[c] = colour[:rows]
        gap = (colour - info[2 + c]) * present
        misfit.append(gap)
        before = before + gap * jnp.where(ascending, mine[c], theirs[c])
    ramp_b[4] = jnp.where(ascending, enter, enter0) * before
    for i in range(4):
        ramp_b[i] = (
            enter * (misfit[0] * coef_s[0, i] + misfit[1] * coef_s[1, i] + misfit[2] * coef_s[2, i]) * (1.0 / 8.0**i)
        )
    share = rows // 2
    for c in range(3):
        image_v[c] = colours[c, pl.ds(pl.multiple_of(core * share, 8), share), :]

    face.wait_send()
    corner.wait_send()
    swap.wait_send()

    @pl.when(has_prev)
    def _():
        for i in range(CHUNKS + 1):
            halo_prev(i).wait_send()

    @pl.when(has_next)
    def _():
        for i in range(CHUNKS + 1):
            halo_next(i).wait_send()


def backward(
    smooth, shade_b, cz_b, cy_b, cx_b, fac_b, edge_b, ramp_b, image_v,
    image_out, grad_out,
    ay_b, qz_b, full_b, total, sems,
):
    slab, rows, cols = total.shape
    ext = rows + 2 * HALO
    step = slab // CHUNKS
    core = lax.axis_index("depth")
    sign = 2 * core - 1
    first = (1 - core) * (slab - 1)

    def chunk_start(i):
        return core * (step * i) + (1 - core) * (slab - step - step * i)

    def rx(value, shift):
        return pltpu.roll(value, shift % cols, 1)

    def ry(value, shift):
        return pltpu.roll(value, shift % ext, 0)

    image_copy = pltpu.make_async_copy(image_v, image_out, sems.at[CHUNKS])
    image_copy.start()
    ramp = [ramp_b[i] for i in range(4)]
    ramp2 = 2.0 * ramp[2]
    ramp3 = 3.0 * ramp[3]

    def pull(k, rest, down=False):
        left = edge_b[k + 2]
        signed = left - edge_b[k + 3]
        weight = jnp.abs(signed)
        here = smooth[k + 3]
        lit = shade_b[k + 2]
        value = ramp[0] + here * (ramp[1] + here * (ramp[2] + here * ramp[3]))
        deriv = ramp[1] + here * (ramp2 + here * ramp3)
        shown = lit * value
        pulled = weight * value
        if down:
            rest = rest + signed * shown
        direct = weight * lit * deriv + (left * shown - rest) * fac_b[k + 2]
        qx = pulled * cx_b[k + 2]
        qy = pulled * cy_b[k + 2]
        ay_b[k + 2] = (ry(qy, 1) - ry(qy, -1)) + (direct + rx(qx, 1) - rx(qx, -1))
        qz_b[k + 2] = pulled * cz_b[k + 2]
        return rest if down else rest - signed * shown

    def gather(k, carry):
        full_b[k + 1] = ay_b[k + 2] + qz_b[k + 1] - qz_b[k + 3]
        return carry

    def spread(k, carry):
        here = full_b[k + 1]
        mid = here[:rows]
        around = 2.0 * mid + full_b[k, pl.ds(0, rows), :] + full_b[k + 2, pl.ds(0, rows), :]
        around = around + (ry(here, 1) + ry(here, -1))[:rows] + (rx(mid, 1) + rx(mid, -1))
        total[first + sign * k] = around
        return carry

    outs = []

    def write(i):
        start = chunk_start(i)
        out = pltpu.make_async_copy(total.at[pl.ds(start, step)], grad_out.at[pl.ds(start, step)], sems.at[i])
        out.start()
        outs.append(out)

    rest = ramp_b[4]
    pull(-2, pull(-1, rest, True), True)
    qz_b[slab + 2] = jnp.zeros((ext, cols), jnp.float32)
    rest = run(0, 2, 2, pull, rest)
    run(-1, 2, 2, gather, 0)
    for i in range(CHUNKS - 1):
        rest = run(step * i + 2, step, step, pull, rest)
        run(step * i + 1, step, step, gather, 0)
        run(step * i, step, step, spread, 0)
        write(i)
    run(slab - step + 2, step - 2, step - 2, pull, rest)
    run(slab - step + 1, step - 1, step - 1, gather, 0)
    full_b[slab + 1] = qz_b[slab + 1]
    run(slab - step, step, step, spread, 0)
    write(CHUNKS - 1)
    image_copy.wait()
    for out in outs:
        out.wait()


def solution(mesh):
    tiles = mesh.shape["tile"]

    def shards(density, absorption, view_dir, target_ids, palette, coef, light):
        slab, rows, cols = density.shape
        ext = rows + 2 * HALO
        f32 = jnp.float32
        cells = (slab + 2, ext, cols)
        scratch = [
            pltpu.VMEM((slab + 2 * HALO, ext, cols), f32),
            pltpu.VMEM((5, ext, cols), f32),
            pltpu.VMEM(cells, f32),
            pltpu.VMEM(cells, f32),
            pltpu.VMEM(target_ids.shape, jnp.int32),
            pltpu.VMEM(palette.shape, f32),
            pltpu.SMEM(view_dir.shape, jnp.int32),
            pltpu.SMEM(coef.shape, f32),
            pltpu.SMEM(light.shape, f32),
            pltpu.VMEM((4, ext, cols), f32),
            pltpu.VMEM((4, ext, cols), f32),
            pltpu.VMEM((3, rows, cols), f32),
            pltpu.SemaphoreType.DMA,
            pltpu.SemaphoreType.DMA((6,)),
            pltpu.SemaphoreType.DMA((2, CHUNKS + 1)),
            pltpu.SemaphoreType.DMA((2, CHUNKS + 1)),
            pltpu.SemaphoreType.DMA((3,)),
            pltpu.SemaphoreType.DMA((3,)),
        ]
        args = (density, absorption, view_dir, target_ids, palette, coef, light)
        fields = pl.pallas_call(
            functools.partial(forward, tiles, slab, rows, cols, 2 * slab),
            out_shape=(
                pltpu.VMEM((slab + 4, ext, cols), f32),
                *[pltpu.VMEM(cells, f32)] * 5,
                pltpu.VMEM((slab + 3, ext, cols), f32),
                pltpu.VMEM((5, ext, cols), f32),
                pltpu.VMEM((3, rows // 2, cols), f32),
            ),
            in_specs=[pl.BlockSpec(memory_space=pl.ANY)] * 7,
            out_specs=[pl.BlockSpec(memory_space=pltpu.VMEM)] * 9,
            scratch_shapes=scratch,
            compiler_params=pltpu.CompilerParams(
                collective_id=0, has_side_effects=True, vmem_limit_bytes=16 * 1024 * 1024
            ),
        )(*[pltpu.with_memory_space_constraint(x, pltpu.HBM) for x in args])
        return pl.pallas_call(
            backward,
            out_shape=(jax.ShapeDtypeStruct((3, rows // 2, cols), f32), jax.ShapeDtypeStruct(density.shape, f32)),
            in_specs=[pl.BlockSpec(memory_space=pltpu.VMEM)] * 9,
            out_specs=[pl.BlockSpec(memory_space=pl.ANY)] * 2,
            scratch_shapes=[
                pltpu.VMEM(cells, f32),
                pltpu.VMEM((slab + 3, ext, cols), f32),
                pltpu.VMEM((slab + 2, ext, cols), f32),
                pltpu.VMEM(density.shape, f32),
                pltpu.SemaphoreType.DMA((CHUNKS + 1,)),
            ],
            compiler_params=pltpu.CompilerParams(vmem_limit_bytes=16 * 1024 * 1024),
        )(*fields)

    placed = (P("depth", "tile", None), P("tile", None), P("tile"), P("tile", None), P(), P(), P())
    return jax.shard_map(
        shards,
        mesh=mesh,
        in_specs=placed,
        out_specs=(P(None, ("tile", "depth"), None), P("depth", "tile", None)),
        check_vma=False,
    )
```

```python
import functools
import math

import jax
import jax.numpy as jnp
from jax import lax
from jax.experimental import pallas as pl
from jax.experimental.pallas import tpu as pltpu
from jax.sharding import PartitionSpec as P

MESH = pl.DeviceIdType.MESH
LOG2E = math.log2(math.e)
CUTS = (0, 4, 12, 20, 28, 32)
CHUNKS = len(CUTS) - 1
PARTS = 4
HALO = 4


def run(lo, count, unroll, one, carry):
    def several(j, carry):
        for u in range(unroll):
            carry = one(lo + j * unroll + u, carry)
        return carry

    return lax.fori_loop(0, count // unroll, several, carry)


def grouped(layers, group, one, carry):
    layers = list(layers)
    for at in range(0, len(layers), group):
        stores = []
        for k in layers[at : at + group]:
            carry, more = one(k, carry)
            stores += more
        for ref, index, value in stores:
            ref[index] = value
    return carry


def forward(
    tiles, slab, rows, cols, depth_count,
    density, absorption, view_dir, target_ids, palette, coef, light,
    smooth, shade_b, cz_b, cy_b, cx_b, fac_b, gain_b, ramp_b, image_v,
    field, info, edge_b, plus_b, inv_b, ids_v, pal_v, view_s, coef_s, light_s, mine, theirs, colours,
    load_sem, small_sem, halo_send, halo_recv, core_send, core_recv,
):
    tile = lax.axis_index("tile")
    core = lax.axis_index("depth")
    other = 1 - core
    has_prev = tile > 0
    has_next = tile < tiles - 1
    ext = rows + 2 * HALO
    cuts = [slab * cut // 32 for cut in CUTS]
    sign = 2 * core - 1
    first = (1 - core) * (slab - 1)

    def layer(k):
        return first + sign * k

    def chunk(i):
        return core * cuts[i] + other * (slab - cuts[i + 1]), cuts[i + 1] - cuts[i]

    prev_id = (jnp.maximum(tile - 1, 0), core)
    next_id = (jnp.minimum(tile + 1, tiles - 1), core)
    across_id = (tile, other)

    def rx(value, shift):
        return pltpu.roll(value, shift % cols, 1)

    def ry(value, shift):
        return pltpu.roll(value, shift % ext, 0)

    barrier = pltpu.get_barrier_semaphore()
    pl.semaphore_signal(barrier, inc=1, device_id=across_id, device_id_type=MESH)

    @pl.when(has_prev)
    def _():
        pl.semaphore_signal(barrier, inc=1, device_id=prev_id, device_id_type=MESH)

    @pl.when(has_next)
    def _():
        pl.semaphore_signal(barrier, inc=1, device_id=next_id, device_id_type=MESH)

    own = pltpu.make_async_copy(density, field.at[pl.ds(HALO, slab), pl.ds(0, rows), :], load_sem)
    smalls = [
        pltpu.make_async_copy(src, dst, small_sem.at[n])
        for n, (src, dst) in enumerate(
            [
                (view_dir, view_s),
                (absorption, info.at[0, pl.ds(0, rows), :]),
                (light, light_s),
                (coef, coef_s),
                (target_ids, ids_v),
                (palette, pal_v),
            ]
        )
    ]
    for copy in smalls:
        copy.start()
    own.start()

    field[HALO + layer(slab)] = jnp.zeros((ext, cols), jnp.float32)

    def clear_rows(at):
        def clear(j, carry):
            field[HALO + j, pl.ds(at, HALO), :] = jnp.zeros((HALO, cols), jnp.float32)
            return carry

        lax.fori_loop(0, slab, clear, 0)
        for n in range(5):
            info[n, pl.ds(at, HALO), :] = jnp.zeros((HALO, cols), jnp.float32)

    @pl.when(jnp.logical_not(has_prev))
    def _():
        clear_rows(rows + HALO)

    @pl.when(jnp.logical_not(has_next))
    def _():
        clear_rows(rows)

    pl.semaphore_wait(barrier, 1 + has_prev.astype(jnp.int32) + has_next.astype(jnp.int32))

    def across(src, dst, n):
        return pltpu.make_async_remote_copy(
            src, dst, core_send.at[n], core_recv.at[n], device_id=across_id, device_id_type=MESH
        )

    face_at = core * (slab + HALO)
    face = across(
        density.at[pl.ds(other * (slab - HALO), HALO)], field.at[pl.ds(face_at, HALO), pl.ds(0, rows), :], 0
    )
    corner = across(
        field.at[pl.ds(HALO + other * (slab - HALO), HALO), pl.ds(rows, 2 * HALO), :],
        field.at[pl.ds(face_at, HALO), pl.ds(rows, 2 * HALO), :],
        1,
    )

    def to_prev(src, dst, n):
        return pltpu.make_async_remote_copy(
            src, dst, halo_send.at[0, n], halo_recv.at[0, n], device_id=prev_id, device_id_type=MESH
        )

    def to_next(src, dst, n):
        return pltpu.make_async_remote_copy(
            src, dst, halo_send.at[1, n], halo_recv.at[1, n], device_id=next_id, device_id_type=MESH
        )

    low, high = pl.ds(0, HALO), pl.ds(rows - HALO, HALO)
    after, before_rows = pl.ds(rows, HALO), pl.ds(rows + HALO, HALO)

    def halo_prev(i):
        if i == CHUNKS:
            return to_prev(info.at[:, low, :], info.at[:, after, :], i)
        start, step = chunk(i)
        return to_prev(density.at[pl.ds(start, step), low, :], field.at[pl.ds(HALO + start, step), after, :], i)

    def halo_next(i):
        if i == CHUNKS:
            return to_next(info.at[:, high, :], info.at[:, before_rows, :], i)
        start, step = chunk(i)
        return to_next(density.at[pl.ds(start, step), high, :], field.at[pl.ds(HALO + start, step), before_rows, :], i)

    def halo_start(i):
        @pl.when(has_prev)
        def _():
            halo_prev(i).start()

        @pl.when(has_next)
        def _():
            halo_next(i).start()

    def halo_arrived(i):
        @pl.when(has_prev)
        def _():
            halo_next(i).wait_recv()

        @pl.when(has_next)
        def _():
            halo_prev(i).wait_recv()

    halo_start(0)
    face.start()
    for i in range(1, CHUNKS - 2):
        halo_start(i)

    for copy in smalls:
        copy.wait()
    own_row = lax.broadcasted_iota(jnp.int32, (rows, cols), 0)
    view = jnp.zeros((rows, cols), jnp.int32)
    for y in range(rows):
        view = jnp.where(own_row == y, view_s[y], view)
    info[1, pl.ds(0, rows), :] = view.astype(jnp.float32)
    for c in range(3):
        table = jnp.broadcast_to(pal_v[pl.ds(c, 1), :], (8, pal_v.shape[1]))
        for y in range(0, rows, 8):
            for x in range(0, cols, 128):
                picked = jnp.take_along_axis(table, ids_v[pl.ds(y, 8), pl.ds(x, 128)], axis=1, mode="promise_in_bounds")
                info[2 + c, pl.ds(y, 8), pl.ds(x, 128)] = picked
    for i in (CHUNKS, CHUNKS - 2, CHUNKS - 1):
        halo_start(i)
    half_light = [0.5 * light_s[0] * sign.astype(jnp.float32), 0.5 * light_s[1], 0.5 * light_s[2]]

    own.wait()
    halo_arrived(0)
    corner.start()

    def blur(k, carry):
        at = HALO + layer(k)
        here = field[at]
        total = 2.0 * here + field[at - 1] + field[at + 1]
        total = total + (ry(here, 1) + ry(here, -1)) + (rx(here, 1) + rx(here, -1))
        return carry, [(smooth, k + 3, total)]

    def shade(k):
        here = smooth[k + 3]
        dz = smooth[k + 4] - smooth[k + 2]
        dy = ry(here, -1) - ry(here, 1)
        dx = rx(here, -1) - rx(here, 1)
        inv = lax.rsqrt(256.0 + dz * dz + dy * dy + dx * dx)
        facing = (half_light[0] * dz + half_light[1] * dy + half_light[2] * dx) * inv
        plus = jnp.log(1.0 + lax.exp2(here * (LOG2E / 8.0)))
        at = k + 2
        return plus, [
            (shade_b, at, 0.5 + facing), (cz_b, at, dz), (cy_b, at, dy), (cx_b, at, dx), (inv_b, at, inv), (plus_b, at, plus)
        ]

    def shade_up(k, depth):
        plus, stores = shade(k)
        return depth + plus, [(edge_b, k + 2, depth), *stores]

    def shade_down(k, depth):
        plus, stores = shade(k)
        return depth - plus, [(edge_b, k + 2, depth - plus), *stores]

    zero = jnp.zeros((ext, cols), jnp.float32)
    def composite(lo, hi, toward, base, sums):
        left = lax.exp2(toward * edge_b[lo + 2] + base)
        m0, m1, m2, m3 = sums
        for k in range(lo, hi):
            right = lax.exp2(toward * edge_b[k + 3] + base)
            here = smooth[k + 3]
            part = jnp.abs(left - right) * shade_b[k + 2]
            m0 = m0 + part
            part = part * here
            m1 = m1 + part
            part = part * here
            m2 = m2 + part
            part = part * here
            m3 = m3 + part
            left = right
        return m0, m1, m2, m3

    def composite_more(lo, hi, start, end, sums):
        dim = jnp.where(ascending, 1.0, lax.exp2((start - end) * scale))
        edge_b[hi + 2] = end
        return composite(lo, hi, toward, jnp.where(ascending, 0.0, -end) * scale, [m * dim for m in sums])

    far = zero
    blurred, shaded, summed = 1, 2, 2
    start = zero
    sums = [zero] * 4
    for i in range(1, CHUNKS):
        last = i == CHUNKS - 1
        if last:
            face.wait_recv()
            corner.wait_recv()
            grouped((0, -1, -2, -3), 4, blur, 0)
            near = grouped((1, 0), 2, shade_down, zero)
            grouped((-1, -2), 2, shade_down, near)
            near_sums = composite(0, 2, toward, jnp.where(ascending, near, 0.0) * scale, [zero] * 4)
        halo_arrived(i)
        reach = slab if last else cuts[i + 1] - 1
        grouped(range(blurred, reach), 4, blur, 0)
        if last:
            smooth[slab + 3] = field[HALO + layer(slab - 1)]
        blurred = reach
        reach = slab if last else reach - 1
        far = grouped(range(shaded, reach), 2, shade_up, far)
        shaded = reach
        if i == CHUNKS - 3:
            halo_arrived(CHUNKS)
            absorb = info[0]
            ascending = info[1] == other.astype(jnp.float32)
            scale = absorb * (LOG2E / depth_count)
            slope = absorb * (1.0 / (8.0 * depth_count))
            toward = jnp.where(ascending, -scale, scale)
        if i >= CHUNKS - 3:
            sums = composite_more(summed, shaded, start, far, sums)
            summed, start = shaded, far

    near_dim = jnp.where(ascending, 1.0, lax.exp2(-far * scale))
    far_dim = jnp.where(ascending, lax.exp2(near * scale), 1.0)
    m0, m1, m2, m3 = [near_dim * m + far_dim * n for m, n in zip(near_sums, sums)]
    base = jnp.where(ascending, near, -far) * scale
    depth = (far - near) * scale
    for c in range(3):
        mine[c] = coef_s[c, 0] * m0 + (coef_s[c, 1] / 8.0) * m1 + (coef_s[c, 2] / 64.0) * m2 + (coef_s[c, 3] / 512.0) * m3
    mine[3] = depth
    swap = across(mine, theirs, 2)
    swap.start()

    side = jnp.where(ascending, 1.0, -1.0)
    slope = side * slope

    def bend(k, left):
        right = lax.exp2(toward * edge_b[k + 3] + base)
        weight = jnp.abs(left - right)
        lit = shade_b[k + 2]
        inv = inv_b[k + 2]
        turn = (lit - 0.5) * inv
        bright = weight * inv
        cz_b[k + 2] = bright * (half_light[0] - turn * cz_b[k + 2])
        cy_b[k + 2] = bright * (half_light[1] - turn * cy_b[k + 2])
        cx_b[k + 2] = bright * (half_light[2] - turn * cx_b[k + 2])
        fac = slope * lax.exp2(smooth[k + 3] * (LOG2E / 8.0) - plus_b[k + 2] * LOG2E)
        fac_b[k + 2] = fac
        gain_b[k + 2] = side * (left * lit) * fac
        shade_b[k + 2] = weight * lit
        return right

    left = run(-2, slab, 8, bend, lax.exp2(toward * edge_b[0] + base))
    run(slab - 2, 2, 2, bend, left)
    enter0 = lax.exp2(-depth)
    swap.wait_recv()

    enter = jnp.where(ascending, lax.exp2(-theirs[3]), 1.0)
    row = lax.broadcasted_iota(jnp.int32, (ext, cols), 0)
    present = jnp.where(row < rows, 1.0, jnp.where(row < rows + HALO, has_next.astype(jnp.float32), has_prev.astype(jnp.float32)))
    present = present * float(depth_count)
    misfit = []
    before = zero
    for c in range(3):
        colour = jnp.where(ascending, theirs[c] + enter * mine[c], mine[c] + enter0 * theirs[c])
        colours[c] = colour[:rows]
        gap = (colour - info[2 + c]) * present
        misfit.append(gap)
        before = before + gap * jnp.where(ascending, mine[c], theirs[c])
    ramp_b[4] = jnp.where(ascending, enter, -enter0) * before
    for i in range(4):
        ramp_b[i] = (
            enter * (misfit[0] * coef_s[0, i] + misfit[1] * coef_s[1, i] + misfit[2] * coef_s[2, i]) * (1.0 / 8.0**i)
        )
    share = rows // 2
    for c in range(3):
        image_v[c] = colours[c, pl.ds(pl.multiple_of(core * share, 8), share), :]

    face.wait_send()
    corner.wait_send()
    swap.wait_send()

    @pl.when(has_prev)
    def _():
        for i in range(CHUNKS + 1):
            halo_prev(i).wait_send()

    @pl.when(has_next)
    def _():
        for i in range(CHUNKS + 1):
            halo_next(i).wait_send()


def backward(
    smooth, lit_b, cz_b, cy_b, cx_b, fac_b, gain_b, ramp_b, image_v,
    image_out, grad_out,
    ay_b, qz_b, full_b, total, sems,
):
    slab, rows, cols = total.shape
    ext = rows + 2 * HALO
    step = slab // PARTS
    core = lax.axis_index("depth")
    sign = 2 * core - 1
    first = (1 - core) * (slab - 1)

    def chunk_start(i):
        return core * (step * i) + (1 - core) * (slab - step - step * i)

    def rx(value, shift):
        return pltpu.roll(value, shift % cols, 1)

    def ry(value, shift):
        return pltpu.roll(value, shift % ext, 0)

    image_copy = pltpu.make_async_copy(image_v, image_out, sems.at[PARTS])
    image_copy.start()
    ramp = [ramp_b[i] for i in range(4)]
    ramp2 = 2.0 * ramp[2]
    ramp3 = 3.0 * ramp[3]

    def pull(k, rest, down=False):
        here = smooth[k + 3]
        lit = lit_b[k + 2]
        value = ramp[0] + here * (ramp[1] + here * (ramp[2] + here * ramp[3]))
        deriv = ramp[1] + here * (ramp2 + here * ramp3)
        shown = lit * value
        if down:
            rest = rest + shown
        direct = lit * deriv + (gain_b[k + 2] * value - rest * fac_b[k + 2])
        qx = value * cx_b[k + 2]
        qy = value * cy_b[k + 2]
        stores = [
            (ay_b, k + 2, (ry(qy, 1) - ry(qy, -1)) + (direct + rx(qx, 1) - rx(qx, -1))),
            (qz_b, k + 2, value * cz_b[k + 2]),
        ]
        return rest if down else rest - shown, stores

    def pull_down(k, rest):
        return pull(k, rest, True)

    def gather(k, carry):
        return carry, [(full_b, k + 1, ay_b[k + 2] + qz_b[k + 1] - qz_b[k + 3])]

    def spread(k, carry):
        here = full_b[k + 1]
        mid = here[:rows]
        around = 2.0 * mid + full_b[k, pl.ds(0, rows), :] + full_b[k + 2, pl.ds(0, rows), :]
        around = around + (ry(here, 1) + ry(here, -1))[:rows] + (rx(mid, 1) + rx(mid, -1))
        return carry, [(total, first + sign * k, around)]

    outs = []

    def write(i):
        start = chunk_start(i)
        out = pltpu.make_async_copy(total.at[pl.ds(start, step)], grad_out.at[pl.ds(start, step)], sems.at[i])
        out.start()
        outs.append(out)

    rest = ramp_b[4]
    grouped((-1, -2), 2, pull_down, rest)
    qz_b[slab + 2] = jnp.zeros((ext, cols), jnp.float32)
    done = 0
    for i in range(PARTS):
        last = i == PARTS - 1
        reach = slab if last else step * (i + 1) + 2
        rest = grouped(range(done, reach), 2, pull, rest)
        grouped(range(done - 1, slab if last else reach - 1), 4, gather, 0)
        done = reach
        if last:
            full_b[slab + 1] = qz_b[slab + 1]
        grouped(range(step * i, step * (i + 1)), 4, spread, 0)
        write(i)
    image_copy.wait()
    for out in outs:
        out.wait()


def solution(mesh):
    tiles = mesh.shape["tile"]

    def shards(density, absorption, view_dir, target_ids, palette, coef, light):
        slab, rows, cols = density.shape
        ext = rows + 2 * HALO
        f32 = jnp.float32
        cells = (slab + 2, ext, cols)
        scratch = [
            pltpu.VMEM((slab + 2 * HALO, ext, cols), f32),
            pltpu.VMEM((5, ext, cols), f32),
            pltpu.VMEM((slab + 3, ext, cols), f32),
            pltpu.VMEM(cells, f32),
            pltpu.VMEM(cells, f32),
            pltpu.VMEM(target_ids.shape, jnp.int32),
            pltpu.VMEM(palette.shape, f32),
            pltpu.SMEM(view_dir.shape, jnp.int32),
            pltpu.SMEM(coef.shape, f32),
            pltpu.SMEM(light.shape, f32),
            pltpu.VMEM((4, ext, cols), f32),
            pltpu.VMEM((4, ext, cols), f32),
            pltpu.VMEM((3, rows, cols), f32),
            pltpu.SemaphoreType.DMA,
            pltpu.SemaphoreType.DMA((6,)),
            pltpu.SemaphoreType.DMA((2, CHUNKS + 1)),
            pltpu.SemaphoreType.DMA((2, CHUNKS + 1)),
            pltpu.SemaphoreType.DMA((3,)),
            pltpu.SemaphoreType.DMA((3,)),
        ]
        args = (density, absorption, view_dir, target_ids, palette, coef, light)
        fields = pl.pallas_call(
            functools.partial(forward, tiles, slab, rows, cols, 2 * slab),
            out_shape=(
                pltpu.VMEM((slab + 4, ext, cols), f32),
                *[pltpu.VMEM(cells, f32)] * 6,
                pltpu.VMEM((5, ext, cols), f32),
                pltpu.VMEM((3, rows // 2, cols), f32),
            ),
            in_specs=[pl.BlockSpec(memory_space=pl.ANY)] * 7,
            out_specs=[pl.BlockSpec(memory_space=pltpu.VMEM)] * 9,
            scratch_shapes=scratch,
            compiler_params=pltpu.CompilerParams(
                collective_id=0, has_side_effects=True, vmem_limit_bytes=16 * 1024 * 1024
            ),
        )(*[pltpu.with_memory_space_constraint(x, pltpu.HBM) for x in args])
        return pl.pallas_call(
            backward,
            out_shape=(jax.ShapeDtypeStruct((3, rows // 2, cols), f32), jax.ShapeDtypeStruct(density.shape, f32)),
            in_specs=[pl.BlockSpec(memory_space=pltpu.VMEM)] * 9,
            out_specs=[pl.BlockSpec(memory_space=pl.ANY)] * 2,
            scratch_shapes=[
                pltpu.VMEM(cells, f32),
                pltpu.VMEM((slab + 3, ext, cols), f32),
                pltpu.VMEM((slab + 2, ext, cols), f32),
                pltpu.VMEM(density.shape, f32),
                pltpu.SemaphoreType.DMA((PARTS + 1,)),
            ],
            compiler_params=pltpu.CompilerParams(vmem_limit_bytes=16 * 1024 * 1024),
        )(*fields)

    placed = (P("depth", "tile", None), P("tile", None), P("tile"), P("tile", None), P(), P(), P())
    return jax.shard_map(
        shards,
        mesh=mesh,
        in_specs=placed,
        out_specs=(P(None, ("tile", "depth"), None), P("depth", "tile", None)),
        check_vma=False,
    )
```

```python
import functools
import math

import jax
import jax.numpy as jnp
from jax import lax
from jax.experimental import pallas as pl
from jax.experimental.pallas import tpu as pltpu
from jax.sharding import PartitionSpec as P

MESH = pl.DeviceIdType.MESH
LOG2E = math.log2(math.e)
CUTS = (0, 8, 14, 20, 26, 32)
CHUNKS = len(CUTS) - 1
PARTS = 4
HALO = 4


def run(lo, count, unroll, one, carry):
    def several(j, carry):
        for u in range(unroll):
            carry = one(lo + j * unroll + u, carry)
        return carry

    return lax.fori_loop(0, count // unroll, several, carry)


def grouped(layers, group, one, carry):
    layers = list(layers)
    for at in range(0, len(layers), group):
        stores = []
        for k in layers[at : at + group]:
            carry, more = one(k, carry)
            stores += more
        for ref, index, value in stores:
            ref[index] = value
    return carry


def forward(
    tiles, slab, rows, cols, depth_count,
    density, absorption, view_dir, target_ids, palette, coef, light,
    smooth, shade_b, cz_b, cy_b, cx_b, fac_b, gain_b, ramp_b, image_v,
    field, info, edge_b, plus_b, inv_b, ids_v, pal_v, view_s, coef_s, light_s, mine, theirs, colours,
    load_sem, small_sem, halo_send, halo_recv, core_send, core_recv,
):
    tile = lax.axis_index("tile")
    core = lax.axis_index("depth")
    other = 1 - core
    has_prev = tile > 0
    has_next = tile < tiles - 1
    ext = rows + 2 * HALO
    cuts = [slab * cut // 32 for cut in CUTS]
    sign = 2 * core - 1
    first = (1 - core) * (slab - 1)

    def layer(k):
        return first + sign * k

    def chunk(i):
        return core * cuts[i] + other * (slab - cuts[i + 1]), cuts[i + 1] - cuts[i]

    prev_id = (jnp.maximum(tile - 1, 0), core)
    next_id = (jnp.minimum(tile + 1, tiles - 1), core)
    across_id = (tile, other)

    def rx(value, shift):
        return pltpu.roll(value, shift % cols, 1)

    def ry(value, shift):
        return pltpu.roll(value, shift % ext, 0)

    barrier = pltpu.get_barrier_semaphore()
    pl.semaphore_signal(barrier, inc=1, device_id=across_id, device_id_type=MESH)

    @pl.when(has_prev)
    def _():
        pl.semaphore_signal(barrier, inc=1, device_id=prev_id, device_id_type=MESH)

    @pl.when(has_next)
    def _():
        pl.semaphore_signal(barrier, inc=1, device_id=next_id, device_id_type=MESH)

    own = pltpu.make_async_copy(density, field.at[pl.ds(HALO, slab), pl.ds(0, rows), :], load_sem)
    smalls = [
        pltpu.make_async_copy(src, dst, small_sem.at[n])
        for n, (src, dst) in enumerate(
            [
                (view_dir, view_s),
                (absorption, info.at[0, pl.ds(0, rows), :]),
                (light, light_s),
                (coef, coef_s),
                (target_ids, ids_v),
                (palette, pal_v),
            ]
        )
    ]
    for copy in smalls:
        copy.start()
    own.start()

    field[HALO + layer(slab)] = jnp.zeros((ext, cols), jnp.float32)

    def clear_rows(at):
        def clear(j, carry):
            field[HALO + j, pl.ds(at, HALO), :] = jnp.zeros((HALO, cols), jnp.float32)
            return carry

        lax.fori_loop(0, slab, clear, 0)
        for n in range(5):
            info[n, pl.ds(at, HALO), :] = jnp.zeros((HALO, cols), jnp.float32)

    @pl.when(jnp.logical_not(has_prev))
    def _():
        clear_rows(rows + HALO)

    @pl.when(jnp.logical_not(has_next))
    def _():
        clear_rows(rows)

    pl.semaphore_wait(barrier, 1 + has_prev.astype(jnp.int32) + has_next.astype(jnp.int32))

    def across(src, dst, n):
        return pltpu.make_async_remote_copy(
            src, dst, core_send.at[n], core_recv.at[n], device_id=across_id, device_id_type=MESH
        )

    face_at = core * (slab + HALO)
    face = across(
        density.at[pl.ds(other * (slab - HALO), HALO)], field.at[pl.ds(face_at, HALO), pl.ds(0, rows), :], 0
    )
    corner = across(
        field.at[pl.ds(HALO + other * (slab - HALO), HALO), pl.ds(rows, 2 * HALO), :],
        field.at[pl.ds(face_at, HALO), pl.ds(rows, 2 * HALO), :],
        1,
    )

    def to_prev(src, dst, n):
        return pltpu.make_async_remote_copy(
            src, dst, halo_send.at[0, n], halo_recv.at[0, n], device_id=prev_id, device_id_type=MESH
        )

    def to_next(src, dst, n):
        return pltpu.make_async_remote_copy(
            src, dst, halo_send.at[1, n], halo_recv.at[1, n], device_id=next_id, device_id_type=MESH
        )

    low, high = pl.ds(0, HALO), pl.ds(rows - HALO, HALO)
    after, before_rows = pl.ds(rows, HALO), pl.ds(rows + HALO, HALO)

    def halo_prev(i):
        if i == CHUNKS:
            return to_prev(info.at[:, low, :], info.at[:, after, :], i)
        start, step = chunk(i)
        return to_prev(density.at[pl.ds(start, step), low, :], field.at[pl.ds(HALO + start, step), after, :], i)

    def halo_next(i):
        if i == CHUNKS:
            return to_next(info.at[:, high, :], info.at[:, before_rows, :], i)
        start, step = chunk(i)
        return to_next(density.at[pl.ds(start, step), high, :], field.at[pl.ds(HALO + start, step), before_rows, :], i)

    def halo_start(i):
        @pl.when(has_prev)
        def _():
            halo_prev(i).start()

        @pl.when(has_next)
        def _():
            halo_next(i).start()

    def halo_arrived(i):
        @pl.when(has_prev)
        def _():
            halo_next(i).wait_recv()

        @pl.when(has_next)
        def _():
            halo_prev(i).wait_recv()

    halo_start(0)
    face.start()
    for i in range(1, CHUNKS - 2):
        halo_start(i)

    for copy in smalls:
        copy.wait()
    own_row = lax.broadcasted_iota(jnp.int32, (rows, cols), 0)
    view = jnp.zeros((rows, cols), jnp.int32)
    for y in range(rows):
        view = jnp.where(own_row == y, view_s[y], view)
    info[1, pl.ds(0, rows), :] = view.astype(jnp.float32)
    for c in range(3):
        table = jnp.broadcast_to(pal_v[pl.ds(c, 1), :], (8, pal_v.shape[1]))
        for y in range(0, rows, 8):
            for x in range(0, cols, 128):
                picked = jnp.take_along_axis(table, ids_v[pl.ds(y, 8), pl.ds(x, 128)], axis=1, mode="promise_in_bounds")
                info[2 + c, pl.ds(y, 8), pl.ds(x, 128)] = picked
    for i in (CHUNKS, CHUNKS - 2, CHUNKS - 1):
        halo_start(i)
    half_light = [0.5 * light_s[0] * sign.astype(jnp.float32), 0.5 * light_s[1], 0.5 * light_s[2]]

    own.wait()

    def blur(k, carry):
        at = HALO + layer(k)
        here = field[at]
        total = 2.0 * here + field[at - 1] + field[at + 1]
        total = total + (ry(here, 1) + ry(here, -1)) + (rx(here, 1) + rx(here, -1))
        return carry, [(smooth, k + 3, total)]

    row8 = lax.broadcasted_iota(jnp.int32, (8, cols), 0)

    def blur_own(k, carry):
        at = HALO + layer(k)
        here = field[at, pl.ds(0, rows), :]
        tops = [pltpu.roll(here[y : y + 8], 1, 0) for y in range(0, rows, 8)]
        ends = [pltpu.roll(here[y : y + 8], 7, 0) for y in range(0, rows, 8)]
        none = jnp.zeros((8, cols), jnp.float32)
        up = [jnp.where(row8 < 1, before, now) for before, now in zip([none, *tops[:-1]], tops)]
        down = [jnp.where(row8 > 6, after_, now) for after_, now in zip([*ends[1:], none], ends)]
        total = 2.0 * here + field[at - 1, pl.ds(0, rows), :] + field[at + 1, pl.ds(0, rows), :]
        total = total + (rx(here, 1) + rx(here, -1)) + (jnp.concatenate(up, 0) + jnp.concatenate(down, 0))
        return carry, [(smooth, (k + 3, pl.ds(0, rows), slice(None)), total)]

    def blur_halo(k, carry):
        at = HALO + layer(k)
        halo = pl.ds(rows, 2 * HALO)
        here = field[at, halo, :]
        top = pltpu.roll(here, 1, 0)
        end = pltpu.roll(here, 7, 0)
        up = jnp.where(row8 < 1, pltpu.roll(field[at, pl.ds(rows - 8, 8), :], 1, 0), top)
        down = jnp.where(row8 > 6, pltpu.roll(field[at, pl.ds(0, 8), :], 7, 0), end)
        total = 2.0 * here + field[at - 1, halo, :] + field[at + 1, halo, :]
        total = total + (rx(here, 1) + rx(here, -1)) + (up + down)
        low_rows, high_rows = (k + 3, pl.ds(0, 8), slice(None)), (k + 3, pl.ds(rows - 8, 8), slice(None))
        return carry, [
            (smooth, (k + 3, halo, slice(None)), total),
            (smooth, low_rows, smooth[low_rows] + jnp.where(row8 < 1, top, 0.0)),
            (smooth, high_rows, smooth[high_rows] + jnp.where(row8 > 6, end, 0.0)),
        ]

    def shade(k):
        here = smooth[k + 3]
        dz = smooth[k + 4] - smooth[k + 2]
        dy = ry(here, -1) - ry(here, 1)
        dx = rx(here, -1) - rx(here, 1)
        inv = lax.rsqrt(256.0 + dz * dz + dy * dy + dx * dx)
        facing = (half_light[0] * dz + half_light[1] * dy + half_light[2] * dx) * inv
        plus = jnp.log(1.0 + lax.exp2(here * (LOG2E / 8.0)))
        at = k + 2
        return plus, [
            (shade_b, at, 0.5 + facing), (cz_b, at, dz), (cy_b, at, dy), (cx_b, at, dx), (inv_b, at, inv), (plus_b, at, plus)
        ]

    def shade_up(k, depth):
        plus, stores = shade(k)
        return depth + plus, [(edge_b, k + 2, depth), *stores]

    def shade_down(k, depth):
        plus, stores = shade(k)
        return depth - plus, [(edge_b, k + 2, depth - plus), *stores]

    zero = jnp.zeros((ext, cols), jnp.float32)
    def composite(lo, hi, toward, base, sums):
        parts = []
        for y in range(0, ext, 8):
            tile_rows = pl.ds(y, 8)
            way, from_, (m0, m1, m2, m3) = toward[y : y + 8], base[y : y + 8], [m[y : y + 8] for m in sums]
            left = lax.exp2(way * edge_b[lo + 2, tile_rows, :] + from_)
            for k in range(lo, hi):
                right = lax.exp2(way * edge_b[k + 3, tile_rows, :] + from_)
                here = smooth[k + 3, tile_rows, :]
                part = jnp.abs(left - right) * shade_b[k + 2, tile_rows, :]
                m0 = m0 + part
                part = part * here
                m1 = m1 + part
                part = part * here
                m2 = m2 + part
                part = part * here
                m3 = m3 + part
                left = right
            parts.append((m0, m1, m2, m3))
        return [jnp.concatenate([part[j] for part in parts], 0) for j in range(4)]

    def composite_more(lo, hi, start, end, sums):
        dim = jnp.where(ascending, 1.0, lax.exp2((start - end) * scale))
        edge_b[hi + 2] = end
        return composite(lo, hi, toward, jnp.where(ascending, 0.0, -end) * scale, [m * dim for m in sums])

    far = zero
    blurred, shaded, summed = 1, 2, 2
    start = zero
    sums = [zero] * 4
    grouped(range(1, slab), 4, blur_own, 0)
    for i in range(CHUNKS):
        last = i == CHUNKS - 1
        if last:
            face.wait_recv()
            corner.wait_recv()
            grouped((0, -1, -2, -3), 4, blur, 0)
            near = grouped((1, 0), 2, shade_down, zero)
            grouped((-1, -2), 2, shade_down, near)
            near_sums = composite(0, 2, toward, jnp.where(ascending, near, 0.0) * scale, [zero] * 4)
        halo_arrived(i)
        if i == 0:
            corner.start()
        reach = slab if last else cuts[i + 1] - 1
        grouped(range(blurred, reach), 4, blur_halo, 0)
        if last:
            smooth[slab + 3] = field[HALO + layer(slab - 1)]
        blurred = reach
        reach = slab if last else reach - 1
        far = grouped(range(shaded, reach), 2, shade_up, far)
        shaded = reach
        if i == CHUNKS - 3:
            halo_arrived(CHUNKS)
            absorb = info[0]
            ascending = info[1] == other.astype(jnp.float32)
            scale = absorb * (LOG2E / depth_count)
            slope = absorb * (1.0 / (8.0 * depth_count))
            toward = jnp.where(ascending, -scale, scale)
        if i >= CHUNKS - 3:
            sums = composite_more(summed, shaded, start, far, sums)
            summed, start = shaded, far

    near_dim = jnp.where(ascending, 1.0, lax.exp2(-far * scale))
    far_dim = jnp.where(ascending, lax.exp2(near * scale), 1.0)
    m0, m1, m2, m3 = [near_dim * m + far_dim * n for m, n in zip(near_sums, sums)]
    base = jnp.where(ascending, near, -far) * scale
    depth = (far - near) * scale
    for c in range(3):
        mine[c] = coef_s[c, 0] * m0 + (coef_s[c, 1] / 8.0) * m1 + (coef_s[c, 2] / 64.0) * m2 + (coef_s[c, 3] / 512.0) * m3
    mine[3] = depth
    swap = across(mine, theirs, 2)
    swap.start()

    side = jnp.where(ascending, 1.0, -1.0)
    slope = side * slope

    for y in range(0, ext, 8):
        tile_rows = pl.ds(y, 8)
        way, from_, slope_y, side_y = toward[y : y + 8], base[y : y + 8], slope[y : y + 8], side[y : y + 8]

        def bend(k, left, tile_rows=tile_rows, way=way, from_=from_, slope_y=slope_y, side_y=side_y):
            right = lax.exp2(way * edge_b[k + 3, tile_rows, :] + from_)
            cell = (k + 2, tile_rows, slice(None))
            weight = jnp.abs(left - right)
            lit = shade_b[cell]
            inv = inv_b[cell]
            turn = (lit - 0.5) * inv
            bright = weight * inv
            cz_b[cell] = bright * (half_light[0] - turn * cz_b[cell])
            cy_b[cell] = bright * (half_light[1] - turn * cy_b[cell])
            cx_b[cell] = bright * (half_light[2] - turn * cx_b[cell])
            fac = slope_y * lax.exp2(smooth[k + 3, tile_rows, :] * (LOG2E / 8.0) - plus_b[cell] * LOG2E)
            fac_b[cell] = fac
            gain_b[cell] = side_y * (left * lit) * fac
            shade_b[cell] = weight * lit
            return right

        left = run(-2, slab, 16, bend, lax.exp2(way * edge_b[0, tile_rows, :] + from_))
        run(slab - 2, 2, 2, bend, left)
    enter0 = lax.exp2(-depth)
    swap.wait_recv()

    enter = jnp.where(ascending, lax.exp2(-theirs[3]), 1.0)
    row = lax.broadcasted_iota(jnp.int32, (ext, cols), 0)
    present = jnp.where(row < rows, 1.0, jnp.where(row < rows + HALO, has_next.astype(jnp.float32), has_prev.astype(jnp.float32)))
    present = present * float(depth_count)
    misfit = []
    before = zero
    for c in range(3):
        colour = jnp.where(ascending, theirs[c] + enter * mine[c], mine[c] + enter0 * theirs[c])
        colours[c] = colour[:rows]
        gap = (colour - info[2 + c]) * present
        misfit.append(gap)
        before = before + gap * jnp.where(ascending, mine[c], theirs[c])
    ramp_b[4] = jnp.where(ascending, enter, -enter0) * before
    for i in range(4):
        ramp_b[i] = (
            enter * (misfit[0] * coef_s[0, i] + misfit[1] * coef_s[1, i] + misfit[2] * coef_s[2, i]) * (1.0 / 8.0**i)
        )
    share = rows // 2
    for c in range(3):
        image_v[c] = colours[c, pl.ds(pl.multiple_of(core * share, 8), share), :]

    face.wait_send()
    corner.wait_send()
    swap.wait_send()

    @pl.when(has_prev)
    def _():
        for i in range(CHUNKS + 1):
            halo_prev(i).wait_send()

    @pl.when(has_next)
    def _():
        for i in range(CHUNKS + 1):
            halo_next(i).wait_send()


def lay(ref, at, value):
    rows, cols = value.shape[0] - 8, value.shape[1]
    stores = []
    for h in range(cols // 128):
        lanes = value[:, 128 * h : 128 * h + 128]
        stores.append((ref, (at, h, pl.ds(8, rows), slice(None)), lanes[:rows]))
        stores.append((ref, (at, h, pl.ds(0, 8), slice(None)), lanes[rows:]))
        stores.append((ref, (at, h, pl.ds(rows + 8, 8), slice(None)), lanes[rows:]))
    return stores


def own_rows(ref, at, rows, shift):
    return jnp.concatenate([ref[at, h, pl.ds(8 + shift, rows), :] for h in range(ref.shape[1])], 1)


def halo_rows(ref, at, rows, shift):
    start = 8 + rows + shift if shift < 0 else shift
    return jnp.concatenate([ref[at, h, pl.ds(start, 8), :] for h in range(ref.shape[1])], 1)


def backward(
    smooth, lit_b, cz_b, cy_b, cx_b, fac_b, gain_b, ramp_b, image_v,
    image_out, grad_out,
    ay_b, qz_b, qy_b, full_b, total, sems,
):
    slab, rows, cols = total.shape
    ext = rows + 2 * HALO
    step = slab // PARTS
    core = lax.axis_index("depth")
    sign = 2 * core - 1
    first = (1 - core) * (slab - 1)

    def chunk_start(i):
        return core * (step * i) + (1 - core) * (slab - step - step * i)

    def rx(value, shift):
        return pltpu.roll(value, shift % cols, 1)

    image_copy = pltpu.make_async_copy(image_v, image_out, sems.at[PARTS])
    image_copy.start()
    def puller(y, down=False):
        tile_rows = pl.ds(y, 8)
        ramp = [ramp_b[i, tile_rows, :] for i in range(4)]
        ramp2 = 2.0 * ramp[2]
        ramp3 = 3.0 * ramp[3]
        places = [8 + y] if y < rows else [0, 8 + y]

        def pull(k, rest):
            cell = (k + 2, tile_rows, slice(None))
            here = smooth[k + 3, tile_rows, :]
            lit = lit_b[cell]
            value = ramp[0] + here * (ramp[1] + here * (ramp[2] + here * ramp[3]))
            deriv = ramp[1] + here * (ramp2 + here * ramp3)
            shown = lit * value
            if down:
                rest = rest + shown
            direct = lit * deriv + (gain_b[cell] * value - rest * fac_b[cell])
            qx = value * cx_b[cell]
            qy = value * cy_b[cell]
            stores = [(ay_b, cell, direct + rx(qx, 1) - rx(qx, -1)), (qz_b, cell, value * cz_b[cell])]
            for h in range(cols // 128):
                for place in places:
                    stores.append((qy_b, (k + 2, h, pl.ds(place, 8), slice(None)), qy[:, 128 * h : 128 * h + 128]))
            return rest if down else rest - shown, stores

        return pull

    def gather(k, carry):
        part = ay_b[k + 2] + qz_b[k + 1] - qz_b[k + 3]
        own = own_rows(qy_b, k + 2, rows, -1) - own_rows(qy_b, k + 2, rows, 1)
        halo = halo_rows(qy_b, k + 2, rows, -1) - halo_rows(qy_b, k + 2, rows, 1)
        return carry, lay(full_b, k + 1, part + jnp.concatenate([own, halo], 0))

    def spread(k, carry):
        mid = own_rows(full_b, k + 1, rows, 0)
        around = 2.0 * mid + own_rows(full_b, k, rows, 0) + own_rows(full_b, k + 2, rows, 0)
        around = around + (own_rows(full_b, k + 1, rows, -1) + own_rows(full_b, k + 1, rows, 1)) + (rx(mid, 1) + rx(mid, -1))
        return carry, [(total, first + sign * k, around)]

    outs = []

    def write(i):
        start = chunk_start(i)
        out = pltpu.make_async_copy(total.at[pl.ds(start, step)], grad_out.at[pl.ds(start, step)], sems.at[i])
        out.start()
        outs.append(out)

    rests = {y: ramp_b[4, pl.ds(y, 8), :] for y in range(0, ext, 8)}
    for y, rest in rests.items():
        grouped((-1, -2), 2, puller(y, True), rest)
    qz_b[slab + 2] = jnp.zeros((ext, cols), jnp.float32)
    done = 0
    for i in range(PARTS):
        last = i == PARTS - 1
        reach = slab if last else step * (i + 1) + 2
        for y in rests:
            rests[y] = grouped(range(done, reach), 4, puller(y), rests[y])
        grouped(range(done - 1, slab if last else reach - 1), 4, gather, 0)
        done = reach
        if last:
            for ref, index, value in lay(full_b, slab + 1, qz_b[slab + 1]):
                ref[index] = value
        grouped(range(step * i, step * (i + 1)), 4, spread, 0)
        write(i)
    image_copy.wait()
    for out in outs:
        out.wait()


def solution(mesh):
    tiles = mesh.shape["tile"]

    def shards(density, absorption, view_dir, target_ids, palette, coef, light):
        slab, rows, cols = density.shape
        ext = rows + 2 * HALO
        f32 = jnp.float32
        cells = (slab + 2, ext, cols)
        scratch = [
            pltpu.VMEM((slab + 2 * HALO, ext, cols), f32),
            pltpu.VMEM((5, ext, cols), f32),
            pltpu.VMEM((slab + 3, ext, cols), f32),
            pltpu.VMEM(cells, f32),
            pltpu.VMEM(cells, f32),
            pltpu.VMEM(target_ids.shape, jnp.int32),
            pltpu.VMEM(palette.shape, f32),
            pltpu.SMEM(view_dir.shape, jnp.int32),
            pltpu.SMEM(coef.shape, f32),
            pltpu.SMEM(light.shape, f32),
            pltpu.VMEM((4, ext, cols), f32),
            pltpu.VMEM((4, ext, cols), f32),
            pltpu.VMEM((3, rows, cols), f32),
            pltpu.SemaphoreType.DMA,
            pltpu.SemaphoreType.DMA((6,)),
            pltpu.SemaphoreType.DMA((2, CHUNKS + 1)),
            pltpu.SemaphoreType.DMA((2, CHUNKS + 1)),
            pltpu.SemaphoreType.DMA((3,)),
            pltpu.SemaphoreType.DMA((3,)),
        ]
        args = (density, absorption, view_dir, target_ids, palette, coef, light)
        fields = pl.pallas_call(
            functools.partial(forward, tiles, slab, rows, cols, 2 * slab),
            out_shape=(
                pltpu.VMEM((slab + 4, ext, cols), f32),
                *[pltpu.VMEM(cells, f32)] * 6,
                pltpu.VMEM((5, ext, cols), f32),
                pltpu.VMEM((3, rows // 2, cols), f32),
            ),
            in_specs=[pl.BlockSpec(memory_space=pl.ANY)] * 7,
            out_specs=[pl.BlockSpec(memory_space=pltpu.VMEM)] * 9,
            scratch_shapes=scratch,
            compiler_params=pltpu.CompilerParams(
                collective_id=0, has_side_effects=True, vmem_limit_bytes=16 * 1024 * 1024
            ),
        )(*[pltpu.with_memory_space_constraint(x, pltpu.HBM) for x in args])
        return pl.pallas_call(
            backward,
            out_shape=(jax.ShapeDtypeStruct((3, rows // 2, cols), f32), jax.ShapeDtypeStruct(density.shape, f32)),
            in_specs=[pl.BlockSpec(memory_space=pltpu.VMEM)] * 9,
            out_specs=[pl.BlockSpec(memory_space=pl.ANY)] * 2,
            scratch_shapes=[
                pltpu.VMEM(cells, f32),
                pltpu.VMEM((slab + 3, ext, cols), f32),
                pltpu.VMEM((slab + 2, cols // 128, rows + 16, 128), f32),
                pltpu.VMEM((slab + 2, cols // 128, rows + 16, 128), f32),
                pltpu.VMEM(density.shape, f32),
                pltpu.SemaphoreType.DMA((PARTS + 1,)),
            ],
            compiler_params=pltpu.CompilerParams(vmem_limit_bytes=16 * 1024 * 1024),
        )(*fields)

    placed = (P("depth", "tile", None), P("tile", None), P("tile"), P("tile", None), P(), P(), P())
    return jax.shard_map(
        shards,
        mesh=mesh,
        in_specs=placed,
        out_specs=(P(None, ("tile", "depth"), None), P("depth", "tile", None)),
        check_vma=False,
    )
```

```python
import functools
import math

import jax
import jax.numpy as jnp
from jax import lax
from jax.experimental import pallas as pl
from jax.experimental.pallas import tpu as pltpu
from jax.sharding import PartitionSpec as P

MESH = pl.DeviceIdType.MESH
LOG2E = math.log2(math.e)
CUTS = (0, 4, 10, 16, 22, 28, 32)
CHUNKS = len(CUTS) - 1
PARTS = 4
HALO = 4


def run(lo, count, unroll, one, carry):
    def several(j, carry):
        for u in range(unroll):
            carry = one(lo + j * unroll + u, carry)
        return carry

    return lax.fori_loop(0, count // unroll, several, carry)


def grouped(layers, group, one, carry):
    layers = list(layers)
    for at in range(0, len(layers), group):
        stores = []
        for k in layers[at : at + group]:
            carry, more = one(k, carry)
            stores += more
        for ref, index, value in stores:
            ref[index] = value
    return carry


def forward(
    tiles, slab, rows, cols, depth_count,
    density, absorption, view_dir, target_ids, palette, coef, light,
    smooth, shade_b, cz_b, cy_b, cx_b, fac_b, gain_b, ramp_b, image_v,
    field, info, edge_b, plus_b, inv_b, ids_v, pal_v, view_s, coef_s, light_s, mine, theirs, colours,
    load_sem, small_sem, halo_send, halo_recv, core_send, core_recv,
):
    tile = lax.axis_index("tile")
    core = lax.axis_index("depth")
    other = 1 - core
    has_prev = tile > 0
    has_next = tile < tiles - 1
    ext = rows + 2 * HALO
    cuts = [slab * cut // 32 for cut in CUTS]
    sign = 2 * core - 1
    first = (1 - core) * (slab - 1)

    def layer(k):
        return first + sign * k

    def chunk(i):
        return core * cuts[i] + other * (slab - cuts[i + 1]), cuts[i + 1] - cuts[i]

    prev_id = (jnp.maximum(tile - 1, 0), core)
    next_id = (jnp.minimum(tile + 1, tiles - 1), core)
    across_id = (tile, other)

    def rx(value, shift):
        return pltpu.roll(value, shift % cols, 1)

    def ry(value, shift):
        return pltpu.roll(value, shift % ext, 0)

    barrier = pltpu.get_barrier_semaphore()
    pl.semaphore_signal(barrier, inc=1, device_id=across_id, device_id_type=MESH)

    @pl.when(has_prev)
    def _():
        pl.semaphore_signal(barrier, inc=1, device_id=prev_id, device_id_type=MESH)

    @pl.when(has_next)
    def _():
        pl.semaphore_signal(barrier, inc=1, device_id=next_id, device_id_type=MESH)

    own = pltpu.make_async_copy(density, field.at[pl.ds(HALO, slab), pl.ds(0, rows), :], load_sem)
    smalls = [
        pltpu.make_async_copy(src, dst, small_sem.at[n])
        for n, (src, dst) in enumerate(
            [
                (view_dir, view_s),
                (absorption, info.at[0, pl.ds(0, rows), :]),
                (light, light_s),
                (coef, coef_s),
                (target_ids, ids_v),
                (palette, pal_v),
            ]
        )
    ]
    for copy in smalls:
        copy.start()
    own.start()

    field[HALO + layer(slab)] = jnp.zeros((ext, cols), jnp.float32)

    def clear_rows(at):
        def clear(j, carry):
            field[HALO + j, pl.ds(at, HALO), :] = jnp.zeros((HALO, cols), jnp.float32)
            return carry

        lax.fori_loop(0, slab, clear, 0)
        for n in range(5):
            info[n, pl.ds(at, HALO), :] = jnp.zeros((HALO, cols), jnp.float32)

    pl.semaphore_wait(barrier, 1 + has_prev.astype(jnp.int32) + has_next.astype(jnp.int32))

    def across(src, dst, n):
        return pltpu.make_async_remote_copy(
            src, dst, core_send.at[n], core_recv.at[n], device_id=across_id, device_id_type=MESH
        )

    face_at = core * (slab + HALO)
    face = across(
        density.at[pl.ds(other * (slab - HALO), HALO)], field.at[pl.ds(face_at, HALO), pl.ds(0, rows), :], 0
    )
    corner = across(
        field.at[pl.ds(HALO + other * (slab - HALO), HALO), pl.ds(rows, 2 * HALO), :],
        field.at[pl.ds(face_at, HALO), pl.ds(rows, 2 * HALO), :],
        1,
    )

    def to_prev(src, dst, n):
        return pltpu.make_async_remote_copy(
            src, dst, halo_send.at[0, n], halo_recv.at[0, n], device_id=prev_id, device_id_type=MESH
        )

    def to_next(src, dst, n):
        return pltpu.make_async_remote_copy(
            src, dst, halo_send.at[1, n], halo_recv.at[1, n], device_id=next_id, device_id_type=MESH
        )

    low, high = pl.ds(0, HALO), pl.ds(rows - HALO, HALO)
    after, before_rows = pl.ds(rows, HALO), pl.ds(rows + HALO, HALO)

    def halo_prev(i):
        if i == CHUNKS:
            return to_prev(info.at[:, low, :], info.at[:, after, :], i)
        start, step = chunk(i)
        return to_prev(density.at[pl.ds(start, step), low, :], field.at[pl.ds(HALO + start, step), after, :], i)

    def halo_next(i):
        if i == CHUNKS:
            return to_next(info.at[:, high, :], info.at[:, before_rows, :], i)
        start, step = chunk(i)
        return to_next(density.at[pl.ds(start, step), high, :], field.at[pl.ds(HALO + start, step), before_rows, :], i)

    def halo_start(i):
        @pl.when(has_prev)
        def _():
            halo_prev(i).start()

        @pl.when(has_next)
        def _():
            halo_next(i).start()

    def halo_arrived(i):
        @pl.when(has_prev)
        def _():
            halo_next(i).wait_recv()

        @pl.when(has_next)
        def _():
            halo_prev(i).wait_recv()

    halo_start(0)
    face.start()
    for i in range(1, CHUNKS - 2):
        halo_start(i)

    @pl.when(jnp.logical_not(has_prev))
    def _():
        clear_rows(rows + HALO)

    @pl.when(jnp.logical_not(has_next))
    def _():
        clear_rows(rows)

    for copy in smalls:
        copy.wait()
    own_row = lax.broadcasted_iota(jnp.int32, (rows, cols), 0)
    view = jnp.zeros((rows, cols), jnp.int32)
    for y in range(rows):
        view = jnp.where(own_row == y, view_s[y], view)
    info[1, pl.ds(0, rows), :] = view.astype(jnp.float32)
    for c in range(3):
        table = jnp.broadcast_to(pal_v[pl.ds(c, 1), :], (8, pal_v.shape[1]))
        for y in range(0, rows, 8):
            for x in range(0, cols, 128):
                picked = jnp.take_along_axis(table, ids_v[pl.ds(y, 8), pl.ds(x, 128)], axis=1, mode="promise_in_bounds")
                info[2 + c, pl.ds(y, 8), pl.ds(x, 128)] = picked
    for i in (CHUNKS, CHUNKS - 2, CHUNKS - 1):
        halo_start(i)
    half_light = [0.5 * light_s[0] * sign.astype(jnp.float32), 0.5 * light_s[1], 0.5 * light_s[2]]

    own.wait()

    def blur(k, carry):
        at = HALO + layer(k)
        here = field[at]
        total = 2.0 * here + field[at - 1] + field[at + 1]
        total = total + (ry(here, 1) + ry(here, -1)) + (rx(here, 1) + rx(here, -1))
        return carry, [(smooth, k + 3, total)]

    row8 = lax.broadcasted_iota(jnp.int32, (8, cols), 0)

    def blur_own(k, carry):
        at = HALO + layer(k)
        here = field[at, pl.ds(0, rows), :]
        tops = [pltpu.roll(here[y : y + 8], 1, 0) for y in range(0, rows, 8)]
        ends = [pltpu.roll(here[y : y + 8], 7, 0) for y in range(0, rows, 8)]
        none = jnp.zeros((8, cols), jnp.float32)
        up = [jnp.where(row8 < 1, before, now) for before, now in zip([none, *tops[:-1]], tops)]
        down = [jnp.where(row8 > 6, after_, now) for after_, now in zip([*ends[1:], none], ends)]
        total = 2.0 * here + field[at - 1, pl.ds(0, rows), :] + field[at + 1, pl.ds(0, rows), :]
        total = total + (rx(here, 1) + rx(here, -1)) + (jnp.concatenate(up, 0) + jnp.concatenate(down, 0))
        return carry, [(smooth, (k + 3, pl.ds(0, rows), slice(None)), total)]

    def blur_halo(k, carry):
        at = HALO + layer(k)
        halo = pl.ds(rows, 2 * HALO)
        here = field[at, halo, :]
        top = pltpu.roll(here, 1, 0)
        end = pltpu.roll(here, 7, 0)
        up = jnp.where(row8 < 1, pltpu.roll(field[at, pl.ds(rows - 8, 8), :], 1, 0), top)
        down = jnp.where(row8 > 6, pltpu.roll(field[at, pl.ds(0, 8), :], 7, 0), end)
        total = 2.0 * here + field[at - 1, halo, :] + field[at + 1, halo, :]
        total = total + (rx(here, 1) + rx(here, -1)) + (up + down)
        low_rows, high_rows = (k + 3, pl.ds(0, 8), slice(None)), (k + 3, pl.ds(rows - 8, 8), slice(None))
        return carry, [
            (smooth, (k + 3, halo, slice(None)), total),
            (smooth, low_rows, smooth[low_rows] + jnp.where(row8 < 1, top, 0.0)),
            (smooth, high_rows, smooth[high_rows] + jnp.where(row8 > 6, end, 0.0)),
        ]

    def shade(k):
        here = smooth[k + 3]
        dz = smooth[k + 4] - smooth[k + 2]
        dy = ry(here, -1) - ry(here, 1)
        dx = rx(here, -1) - rx(here, 1)
        inv = lax.rsqrt(256.0 + dz * dz + dy * dy + dx * dx)
        facing = (half_light[0] * dz + half_light[1] * dy + half_light[2] * dx) * inv
        plus = jnp.log(1.0 + lax.exp2(here * (LOG2E / 8.0)))
        at = k + 2
        return plus, [
            (shade_b, at, 0.5 + facing), (cz_b, at, dz), (cy_b, at, dy), (cx_b, at, dx), (inv_b, at, inv), (plus_b, at, plus)
        ]

    def shade_up(k, depth):
        plus, stores = shade(k)
        return depth + plus, [(edge_b, k + 2, depth), *stores]

    def shade_down(k, depth):
        plus, stores = shade(k)
        return depth - plus, [(edge_b, k + 2, depth - plus), *stores]

    zero = jnp.zeros((ext, cols), jnp.float32)
    def composite(lo, hi, toward, base, sums):
        parts = []
        for y in range(0, ext, 8):
            tile_rows = pl.ds(y, 8)
            way, from_, (m0, m1, m2, m3) = toward[y : y + 8], base[y : y + 8], [m[y : y + 8] for m in sums]
            left = lax.exp2(way * edge_b[lo + 2, tile_rows, :] + from_)
            for k in range(lo, hi):
                right = lax.exp2(way * edge_b[k + 3, tile_rows, :] + from_)
                here = smooth[k + 3, tile_rows, :]
                part = jnp.abs(left - right) * shade_b[k + 2, tile_rows, :]
                m0 = m0 + part
                part = part * here
                m1 = m1 + part
                part = part * here
                m2 = m2 + part
                part = part * here
                m3 = m3 + part
                left = right
            parts.append((m0, m1, m2, m3))
        return [jnp.concatenate([part[j] for part in parts], 0) for j in range(4)]

    def composite_more(lo, hi, start, end, sums):
        dim = jnp.where(ascending, 1.0, lax.exp2((start - end) * scale))
        edge_b[hi + 2] = end
        return composite(lo, hi, toward, jnp.where(ascending, 0.0, -end) * scale, [m * dim for m in sums])

    far = zero
    blurred, shaded, summed = 1, 2, 2
    start = zero
    sums = [zero] * 4
    grouped(range(1, slab), 4, blur_own, 0)
    for i in range(CHUNKS):
        last = i == CHUNKS - 1
        if last:
            face.wait_recv()
            corner.wait_recv()
            grouped((0, -1, -2, -3), 4, blur, 0)
            near = grouped((1, 0), 2, shade_down, zero)
            grouped((-1, -2), 2, shade_down, near)
            near_sums = composite(0, 2, toward, jnp.where(ascending, near, 0.0) * scale, [zero] * 4)
        halo_arrived(i)
        if i == 0:
            corner.start()
        reach = slab if last else cuts[i + 1] - 1
        grouped(range(blurred, reach), 4, blur_halo, 0)
        if last:
            smooth[slab + 3] = field[HALO + layer(slab - 1)]
        blurred = reach
        reach = slab if last else reach - 1
        far = grouped(range(shaded, reach), 2, shade_up, far)
        shaded = reach
        if i == CHUNKS - 3:
            halo_arrived(CHUNKS)
            absorb = info[0]
            ascending = info[1] == other.astype(jnp.float32)
            scale = absorb * (LOG2E / depth_count)
            slope = absorb * (1.0 / (8.0 * depth_count))
            toward = jnp.where(ascending, -scale, scale)
        if i >= CHUNKS - 3:
            sums = composite_more(summed, shaded, start, far, sums)
            summed, start = shaded, far

    near_dim = jnp.where(ascending, 1.0, lax.exp2(-far * scale))
    far_dim = jnp.where(ascending, lax.exp2(near * scale), 1.0)
    m0, m1, m2, m3 = [near_dim * m + far_dim * n for m, n in zip(near_sums, sums)]
    base = jnp.where(ascending, near, -far) * scale
    depth = (far - near) * scale
    for c in range(3):
        mine[c] = coef_s[c, 0] * m0 + (coef_s[c, 1] / 8.0) * m1 + (coef_s[c, 2] / 64.0) * m2 + (coef_s[c, 3] / 512.0) * m3
    mine[3] = depth
    swap = across(mine, theirs, 2)
    swap.start()

    side = jnp.where(ascending, 1.0, -1.0)
    slope = side * slope

    for y in range(0, ext, 8):
        tile_rows = pl.ds(y, 8)
        way, from_, slope_y, side_y = toward[y : y + 8], base[y : y + 8], slope[y : y + 8], side[y : y + 8]

        def bend(k, left, tile_rows=tile_rows, way=way, from_=from_, slope_y=slope_y, side_y=side_y):
            right = lax.exp2(way * edge_b[k + 3, tile_rows, :] + from_)
            cell = (k + 2, tile_rows, slice(None))
            weight = jnp.abs(left - right)
            lit = shade_b[cell]
            inv = inv_b[cell]
            turn = (lit - 0.5) * inv
            bright = weight * inv
            cz_b[cell] = bright * (half_light[0] - turn * cz_b[cell])
            cy_b[cell] = bright * (half_light[1] - turn * cy_b[cell])
            cx_b[cell] = bright * (half_light[2] - turn * cx_b[cell])
            fac = slope_y * lax.exp2(smooth[k + 3, tile_rows, :] * (LOG2E / 8.0) - plus_b[cell] * LOG2E)
            fac_b[cell] = fac
            gain_b[cell] = side_y * (left * lit) * fac
            shade_b[cell] = weight * lit
            return right

        left = run(-2, slab, 16, bend, lax.exp2(way * edge_b[0, tile_rows, :] + from_))
        run(slab - 2, 2, 2, bend, left)
    enter0 = lax.exp2(-depth)
    swap.wait_recv()

    enter = jnp.where(ascending, lax.exp2(-theirs[3]), 1.0)
    row = lax.broadcasted_iota(jnp.int32, (ext, cols), 0)
    present = jnp.where(row < rows, 1.0, jnp.where(row < rows + HALO, has_next.astype(jnp.float32), has_prev.astype(jnp.float32)))
    present = present * float(depth_count)
    misfit = []
    before = zero
    for c in range(3):
        colour = jnp.where(ascending, theirs[c] + enter * mine[c], mine[c] + enter0 * theirs[c])
        colours[c] = colour[:rows]
        gap = (colour - info[2 + c]) * present
        misfit.append(gap)
        before = before + gap * jnp.where(ascending, mine[c], theirs[c])
    ramp_b[4] = jnp.where(ascending, enter, -enter0) * before
    for i in range(4):
        ramp_b[i] = (
            enter * (misfit[0] * coef_s[0, i] + misfit[1] * coef_s[1, i] + misfit[2] * coef_s[2, i]) * (1.0 / 8.0**i)
        )
    share = rows // 2
    for c in range(3):
        image_v[c] = colours[c, pl.ds(pl.multiple_of(core * share, 8), share), :]

    face.wait_send()
    corner.wait_send()
    swap.wait_send()

    @pl.when(has_prev)
    def _():
        for i in range(CHUNKS + 1):
            halo_prev(i).wait_send()

    @pl.when(has_next)
    def _():
        for i in range(CHUNKS + 1):
            halo_next(i).wait_send()


def lay(ref, at, value):
    rows, cols = value.shape[0] - 8, value.shape[1]
    stores = []
    for h in range(cols // 128):
        lanes = value[:, 128 * h : 128 * h + 128]
        stores.append((ref, (at, h, pl.ds(8, rows), slice(None)), lanes[:rows]))
        stores.append((ref, (at, h, pl.ds(0, 8), slice(None)), lanes[rows:]))
        stores.append((ref, (at, h, pl.ds(rows + 8, 8), slice(None)), lanes[rows:]))
    return stores


def own_rows(ref, at, rows, shift):
    return jnp.concatenate([ref[at, h, pl.ds(8 + shift, rows), :] for h in range(ref.shape[1])], 1)


def halo_rows(ref, at, rows, shift):
    start = 8 + rows + shift if shift < 0 else shift
    return jnp.concatenate([ref[at, h, pl.ds(start, 8), :] for h in range(ref.shape[1])], 1)


def backward(
    smooth, lit_b, cz_b, cy_b, cx_b, fac_b, gain_b, ramp_b, image_v,
    image_out, grad_out,
    ay_b, qz_b, qy_b, full_b, total, sems,
):
    slab, rows, cols = total.shape
    ext = rows + 2 * HALO
    step = slab // PARTS
    core = lax.axis_index("depth")
    sign = 2 * core - 1
    first = (1 - core) * (slab - 1)

    def chunk_start(i):
        return core * (step * i) + (1 - core) * (slab - step - step * i)

    def rx(value, shift):
        return pltpu.roll(value, shift % cols, 1)

    image_copy = pltpu.make_async_copy(image_v, image_out, sems.at[PARTS])
    image_copy.start()
    def puller(y, down=False):
        tile_rows = pl.ds(y, 8)
        ramp = [ramp_b[i, tile_rows, :] for i in range(4)]
        ramp2 = 2.0 * ramp[2]
        ramp3 = 3.0 * ramp[3]
        places = [8 + y] if y < rows else [0, 8 + y]

        def pull(k, rest):
            cell = (k + 2, tile_rows, slice(None))
            here = smooth[k + 3, tile_rows, :]
            lit = lit_b[cell]
            value = ramp[0] + here * (ramp[1] + here * (ramp[2] + here * ramp[3]))
            deriv = ramp[1] + here * (ramp2 + here * ramp3)
            shown = lit * value
            if down:
                rest = rest + shown
            direct = lit * deriv + (gain_b[cell] * value - rest * fac_b[cell])
            qx = value * cx_b[cell]
            qy = value * cy_b[cell]
            stores = [(ay_b, cell, direct + rx(qx, 1) - rx(qx, -1)), (qz_b, cell, value * cz_b[cell])]
            for h in range(cols // 128):
                for place in places:
                    stores.append((qy_b, (k + 2, h, pl.ds(place, 8), slice(None)), qy[:, 128 * h : 128 * h + 128]))
            return rest if down else rest - shown, stores

        return pull

    def gather(k, carry):
        part = ay_b[k + 2] + qz_b[k + 1] - qz_b[k + 3]
        own = own_rows(qy_b, k + 2, rows, -1) - own_rows(qy_b, k + 2, rows, 1)
        halo = halo_rows(qy_b, k + 2, rows, -1) - halo_rows(qy_b, k + 2, rows, 1)
        return carry, lay(full_b, k + 1, part + jnp.concatenate([own, halo], 0))

    def spread(k, carry):
        mid = own_rows(full_b, k + 1, rows, 0)
        around = 2.0 * mid + own_rows(full_b, k, rows, 0) + own_rows(full_b, k + 2, rows, 0)
        around = around + (own_rows(full_b, k + 1, rows, -1) + own_rows(full_b, k + 1, rows, 1)) + (rx(mid, 1) + rx(mid, -1))
        return carry, [(total, first + sign * k, around)]

    outs = []

    def write(i):
        start = chunk_start(i)
        out = pltpu.make_async_copy(total.at[pl.ds(start, step)], grad_out.at[pl.ds(start, step)], sems.at[i])
        out.start()
        outs.append(out)

    rests = {y: ramp_b[4, pl.ds(y, 8), :] for y in range(0, ext, 8)}
    for y, rest in rests.items():
        grouped((-1, -2), 2, puller(y, True), rest)
    qz_b[slab + 2] = jnp.zeros((ext, cols), jnp.float32)
    done = 0
    for i in range(PARTS):
        last = i == PARTS - 1
        reach = slab if last else step * (i + 1) + 2
        for y in rests:
            rests[y] = grouped(range(done, reach), 4, puller(y), rests[y])
        grouped(range(done - 1, slab if last else reach - 1), 4, gather, 0)
        done = reach
        if last:
            for ref, index, value in lay(full_b, slab + 1, qz_b[slab + 1]):
                ref[index] = value
        grouped(range(step * i, step * (i + 1)), 4, spread, 0)
        write(i)
    image_copy.wait()
    for out in outs:
        out.wait()


def solution(mesh):
    tiles = mesh.shape["tile"]

    def shards(density, absorption, view_dir, target_ids, palette, coef, light):
        slab, rows, cols = density.shape
        ext = rows + 2 * HALO
        f32 = jnp.float32
        cells = (slab + 2, ext, cols)
        scratch = [
            pltpu.VMEM((slab + 2 * HALO, ext, cols), f32),
            pltpu.VMEM((5, ext, cols), f32),
            pltpu.VMEM((slab + 3, ext, cols), f32),
            pltpu.VMEM(cells, f32),
            pltpu.VMEM(cells, f32),
            pltpu.VMEM(target_ids.shape, jnp.int32),
            pltpu.VMEM(palette.shape, f32),
            pltpu.SMEM(view_dir.shape, jnp.int32),
            pltpu.SMEM(coef.shape, f32),
            pltpu.SMEM(light.shape, f32),
            pltpu.VMEM((4, ext, cols), f32),
            pltpu.VMEM((4, ext, cols), f32),
            pltpu.VMEM((3, rows, cols), f32),
            pltpu.SemaphoreType.DMA,
            pltpu.SemaphoreType.DMA((6,)),
            pltpu.SemaphoreType.DMA((2, CHUNKS + 1)),
            pltpu.SemaphoreType.DMA((2, CHUNKS + 1)),
            pltpu.SemaphoreType.DMA((3,)),
            pltpu.SemaphoreType.DMA((3,)),
        ]
        args = (density, absorption, view_dir, target_ids, palette, coef, light)
        fields = pl.pallas_call(
            functools.partial(forward, tiles, slab, rows, cols, 2 * slab),
            out_shape=(
                pltpu.VMEM((slab + 4, ext, cols), f32),
                *[pltpu.VMEM(cells, f32)] * 6,
                pltpu.VMEM((5, ext, cols), f32),
                pltpu.VMEM((3, rows // 2, cols), f32),
            ),
            in_specs=[pl.BlockSpec(memory_space=pl.ANY)] * 7,
            out_specs=[pl.BlockSpec(memory_space=pltpu.VMEM)] * 9,
            scratch_shapes=scratch,
            compiler_params=pltpu.CompilerParams(
                collective_id=0, has_side_effects=True, vmem_limit_bytes=16 * 1024 * 1024
            ),
        )(*[pltpu.with_memory_space_constraint(x, pltpu.HBM) for x in args])
        return pl.pallas_call(
            backward,
            out_shape=(jax.ShapeDtypeStruct((3, rows // 2, cols), f32), jax.ShapeDtypeStruct(density.shape, f32)),
            in_specs=[pl.BlockSpec(memory_space=pltpu.VMEM)] * 9,
            out_specs=[pl.BlockSpec(memory_space=pl.ANY)] * 2,
            scratch_shapes=[
                pltpu.VMEM(cells, f32),
                pltpu.VMEM((slab + 3, ext, cols), f32),
                pltpu.VMEM((slab + 2, cols // 128, rows + 16, 128), f32),
                pltpu.VMEM((slab + 2, cols // 128, rows + 16, 128), f32),
                pltpu.VMEM(density.shape, f32),
                pltpu.SemaphoreType.DMA((PARTS + 1,)),
            ],
            compiler_params=pltpu.CompilerParams(vmem_limit_bytes=16 * 1024 * 1024),
        )(*fields)

    placed = (P("depth", "tile", None), P("tile", None), P("tile"), P("tile", None), P(), P(), P())
    return jax.shard_map(
        shards,
        mesh=mesh,
        in_specs=placed,
        out_specs=(P(None, ("tile", "depth"), None), P("depth", "tile", None)),
        check_vma=False,
    )
```
